128 devices in a mesh: section: 2 (over core), expert: 32 (over z, y, x_lo), dp: 2 (over x_hi).
Axes of the slice: x: 4 (x_hi: 2, x_lo: 2; x = x_hi * 2 + x_lo), y: 4, z: 4, core: 2. Of those that a mesh axis runs over, the one named last changes fastest.
Arguments:
- hidden_held: bfloat16 [2, 4096, 4096], P('section', 'expert'), may hold values from -6 to 6
- fresh_rows: bfloat16 [1, 4096, 4096], P(None, 'expert'), may hold values from -6 to 6
- doc_held: int32 [2, 4096], P('section', 'expert'), may hold values from 0 to 63, never falling along the last dimension, each value on 1 to 128 neighbouring positions
- doc_fresh: int32 [1, 4096], P(None, 'expert'), may hold values from 0 to 63, never falling along the last dimension, each value on 1 to 128 neighbouring positions
- routes: int32 [2, 2, 4096, 2], P(None, 'section', 'expert'), may hold values from 0 to 31, all different within a row; in each aligned block of 128 rows (0 to 127, 128 to 255, ..., all dimensions but the last counted through in order) at most 12 rows name the same one
- attn_gain: bfloat16 [2, 4096], P('section'), may hold values from 0.25 to 1.75
- query_gain: bfloat16 [2, 4096], P('section'), may hold values from -4 to 4
- key_gain: bfloat16 [2, 4096], P('section'), may hold values from -4 to 4
- ffn_gain: bfloat16 [2, 4096], P('section'), may hold values from 0.25 to 1.75
- router: bfloat16 [2, 4096, 32], P('section'), may hold values from -0.09375 to 0.09375
- weight_in: bfloat16 [2, 32, 4096, 2, 1536], P('section', 'expert', None, None, 'dp'), may hold values from -0.09375 to 0.09375
- weight_out: bfloat16 [2, 32, 1536, 4096], P('section', 'expert', 'dp'), may hold values from -0.15625 to 0.15625
Outputs:
- layer_out: bfloat16 [2, 2, 4096, 4096], P(None, 'section', 'expert')
The draws below stay inside these ranges and needn't reach their ends.
Inputs may be any that keep to these rules, and one draw needn't show every extreme that they name: `doc_held`: ids never fall along a row; every document has at most 128 tokens, and one has exactly 128. `doc_fresh`: ids never fall along a row; every document has at most 128 tokens, and one has exactly 128. `routes`: the 2 experts of a token differ; among the 128 tokens of one device for one step and layer, no expert is chosen more than 12 times, a bound that some block reaches.
All inputs are finite; a program needn't handle non-finite values.
Results may differ from the reference program's by a relative error of at most 0.017.
Values may be sent and summed in bfloat16 or wider, within the bound.
A program may use at most 128 MiB of HBM per device.

```python
import math
import jax
import jax.numpy as jnp
import numpy as np
from jax import lax

D = 4096
HEAD_DIM = 128
EXPERT_HIDDEN = 1536
TOP = 2
TICKS = 2
TOK_DEV = 128
TOKENS = 4096
LAYERS = 2
EXPERTS = 32
CAP = 12
N_EXPERT = 32


def level_of(stream_key, shape, pieces, smallest, high):
    factor_of, own = 1.0, jax.random.fold_in(stream_key, 6)
    for axis_at, blocks in pieces:
        draws = jnp.exp(jax.random.uniform(jax.random.fold_in(own, axis_at), (blocks,), jnp.float32, smallest / len(pieces), high / len(pieces)))
        factor_of = factor_of * jnp.repeat(draws, shape[axis_at] // blocks).reshape([-1 if axis == axis_at else 1 for axis in range(len(shape))])
    return factor_of


def profile(count, total, limit, skew):
    weights = [(1 << 20) // math.isqrt(grade ** skew) + 1 for grade in range(2, count + 1)]
    rest, given = total - limit - (count - 1), [1] * (count - 1)
    while rest > 0:
        free = [i for i in range(count - 1) if given[i] < limit]
        pool, budget = sum([weights[i] for i in free]), rest
        for i in free:
            more = min(limit - given[i], max(1, budget * weights[i] // pool), rest)
            given[i] = given[i] + more
            rest = rest - more
    return np.array([limit] + given)


def uneven(own_key, amount, total, bound, slope):
    if amount == 2:
        one = jax.random.randint(own_key, (), max(1, total - bound), min(bound, total - 1) + 1)
        return jnp.stack([one, total - one])
    tallies = jnp.asarray(profile(amount, total, bound, slope), jnp.int32)
    couples = (amount - 1) // 2
    giver, sink = tallies[1:1 + 2 * couples:2], tallies[2:2 + 2 * couples:2]
    room = jnp.minimum(giver - 1, bound - sink)
    shifted = jax.random.randint(jax.random.fold_in(own_key, 1), (couples,), 0, 1 << 20) % (room + 1)
    tallies = tallies.at[1:1 + 2 * couples:2].set(giver - shifted).at[2:2 + 2 * couples:2].set(sink + shifted)
    return tallies[jax.random.permutation(jax.random.fold_in(own_key, 2), amount)]


def shared_out(rng, own, number, rows, number_of, top, limit, skew):
    sequence = jax.random.permutation(rng, number_of)
    heavy_load, ordinary = load_shares(number_of, rows * top, limit, skew, True), load_shares(number_of, rows * top, limit, skew, False)
    places = jnp.arange(number_of)

    def named(lengths, turn):
        used = int((lengths > 0).sum())
        fixed = max(1, used // 4)
        passed = fixed + (places - fixed + turn * (used - fixed)) % max(1, number_of - fixed)
        return jnp.zeros((number_of,), jnp.int32).at[sequence[jnp.where(places < fixed, places, passed)]].set(jnp.asarray(lengths, jnp.int32))

    lengths = jnp.where(number % 4 == 0, named(heavy_load, number // 4), named(ordinary, number - number // 4 - 1))
    mixed = jax.random.permutation(jax.random.fold_in(own, 3), number_of)
    donor, taker = mixed[0:number_of // 2 * 2:2], mixed[1:number_of // 2 * 2:2]
    room = jnp.minimum(lengths[donor] - 1, limit - lengths[taker]) // 2
    room = jnp.where((donor == sequence[0]) | (taker == sequence[0]) | (lengths[taker] == 0), 0, jnp.maximum(room, 0))
    passed = jax.random.randint(jax.random.fold_in(own, 4), (number_of // 2,), 0, 1 << 20) % (room + 1)
    lengths = lengths.at[donor].add(-passed).at[taker].add(passed)
    items = jnp.searchsorted(jnp.cumsum(lengths), jnp.arange(rows * top), side="right").astype(jnp.int32)
    table = items.reshape(top, rows).T
    table = table[jax.random.permutation(jax.random.fold_in(own, 1), rows)]
    turn = jax.random.randint(jax.random.fold_in(own, 2), (rows, 1), 0, top)
    return jnp.take_along_axis(table, (jnp.arange(top)[None, :] + turn) % top, axis=1)


def load_shares(amount, total, reach, skew, full):
    loads = [(1 << 20) // math.isqrt(standing ** skew) + 1 for standing in range(1, amount + 1)]
    largest = reach if full else min(reach, max(-(-total // amount), total * loads[0] // sum(loads)))
    least = 1 if total - largest >= amount - 1 else 0
    given, surplus = [largest] + [least] * (amount - 1), total - largest - least * (amount - 1)
    while surplus > 0:
        candidates = [i for i in range(1, amount) if given[i] < largest] or [i for i in range(1, amount) if given[i] < reach]
        mass, remaining = sum([loads[i] for i in candidates]), surplus
        for i in candidates:
            extra = min(reach - given[i], max(1, remaining * loads[i] // mass), surplus)
            given[i] = given[i] + extra
            surplus = surplus - extra
    return np.array(given)


def gaussian(key, extent, deviation, most, split=(), kind=jnp.bfloat16):
    drawn = deviation * jax.random.normal(key, extent, jnp.float32)
    if split:
        drawn = drawn * level_of(key, extent, split, -0.22, 0.18)
    return jnp.clip(drawn, -most, most).astype(kind)


def setup_inputs(seed: int = 0) -> dict:
    seeds = jax.random.split(jax.random.key(seed), 13)
    hidden_held = gaussian(seeds[0], (LAYERS, TOKENS, D), 1.0, 6.0, ((0, 2), (1, 32)))
    fresh_rows = gaussian(seeds[1], (TICKS - 1, TOKENS, D), 1.0, 6.0, ((1, 32),))
    doc_held = jax.vmap(lambda own: jnp.searchsorted(jnp.cumsum(uneven(own, 2 * N_EXPERT, TOKENS, TOK_DEV, 1)), jnp.arange(TOKENS), side="right"))(jax.random.split(seeds[2], LAYERS)).reshape((LAYERS, TOKENS)).astype(jnp.int32)
    doc_fresh = jax.vmap(lambda own: jnp.searchsorted(jnp.cumsum(uneven(own, 2 * N_EXPERT, TOKENS, TOK_DEV, 1)), jnp.arange(TOKENS), side="right"))(jax.random.split(seeds[3], (TICKS - 1))).reshape((TICKS - 1, TOKENS)).astype(jnp.int32)
    routes_keys = jax.random.split(jax.random.fold_in(seeds[4], 1), TICKS * LAYERS * TOKENS // TOK_DEV)
    routes_turns = jax.random.permutation(jax.random.fold_in(seeds[4], 3), TICKS * LAYERS * TOKENS // TOK_DEV)
    routes = jax.vmap(lambda own, number: shared_out(jax.random.fold_in(seeds[4], 2), own, number, TOK_DEV, EXPERTS, TOP, CAP, 2))(routes_keys, routes_turns).reshape((TICKS, LAYERS, TOKENS, TOP))
    attn_gain = jnp.clip(1.0 + 0.15 * jax.random.normal(seeds[5], (LAYERS, D), jnp.float32), 0.25, 1.75).astype(jnp.bfloat16)
    query_gain = gaussian(seeds[6], (LAYERS, D), 1.0, 4.0, ((0, 2),))
    key_gain = gaussian(seeds[7], (LAYERS, D), 1.0, 4.0, ((0, 2),))
    ffn_gain = jnp.clip(1.0 + 0.15 * jax.random.normal(seeds[8], (LAYERS, D), jnp.float32), 0.25, 1.75).astype(jnp.bfloat16)
    router = gaussian(seeds[9], (LAYERS, D, EXPERTS), D ** -0.5, 0.09375, ((0, 2),))
    weight_in = gaussian(seeds[10], (LAYERS, EXPERTS, D, 2, EXPERT_HIDDEN), D ** -0.5, 0.09375, ((0, 2), (1, 32), (4, 2)))
    weight_out = gaussian(seeds[11], (LAYERS, EXPERTS, EXPERT_HIDDEN, D), EXPERT_HIDDEN ** -0.5, 0.15625, ((0, 2), (1, 32), (2, 2)))
    return {"hidden_held": hidden_held, "fresh_rows": fresh_rows, "doc_held": doc_held, "doc_fresh": doc_fresh, "routes": routes, "attn_gain": attn_gain, "query_gain": query_gain, "key_gain": key_gain, "ffn_gain": ffn_gain, "router": router, "weight_in": weight_in, "weight_out": weight_out}


def rms_norm(rows, gain):
    wide = rows.astype(jnp.float32)
    return wide * lax.rsqrt(lax.optimization_barrier(jnp.mean(wide * wide, axis=-1, keepdims=True)) + 1e-06) * gain.astype(jnp.float32)

def attention(normed, documents, query_gain, key_gain):
    row_count = normed.shape[0]
    head_count = normed.shape[1] // HEAD_DIM
    queries = (normed.astype(jnp.float32) * query_gain.astype(jnp.float32)).astype(jnp.bfloat16)
    key_rows = (normed.astype(jnp.float32) * key_gain.astype(jnp.float32)).astype(jnp.bfloat16)

    def heads_first(rows):
        return rows.reshape(row_count, head_count, HEAD_DIM).transpose(1, 0, 2)
    places = jnp.arange(row_count, dtype=jnp.int32)
    allowed = (documents[:, None] == documents[None, :]) & (places[None, :] <= places[:, None])

    def one_head(triple):
        query_head, key_head, value_head = triple
        scores = jnp.einsum('qd,kd->qk', query_head.astype(jnp.float32), key_head.astype(jnp.float32)) * HEAD_DIM ** (-0.5)
        scores = jnp.where(allowed, scores, -1e+30)
        scores = scores - lax.optimization_barrier(jnp.max(scores, axis=1, keepdims=True))
        raised = jnp.exp(scores)
        weights = (raised / lax.optimization_barrier(jnp.sum(raised, axis=1, keepdims=True))).astype(jnp.bfloat16)
        return jnp.einsum('qk,kd->qd', weights.astype(jnp.float32), value_head.astype(jnp.float32)).astype(jnp.bfloat16)
    mixed = lax.map(one_head, (heads_first(queries), heads_first(key_rows), heads_first(normed)))
    return mixed.transpose(1, 0, 2).reshape(row_count, -1)

def expert_outputs(moe_in, chosen, weight_in, weight_out):
    labels = jnp.arange(EXPERTS, dtype=jnp.int32)
    member = lax.optimization_barrier(jnp.sum((chosen[:, :, None] == labels).astype(jnp.int32), axis=1, dtype=jnp.int32))
    ranking = jnp.cumsum(member, axis=0, dtype=jnp.int32) - member
    list_size = N_EXPERT * CAP

    def one_expert(triple):
        flags, inward, outward = triple
        picked_index = jnp.nonzero(flags > 0, size=list_size, fill_value=0)[0]
        rows = moe_in[picked_index]
        projected = jnp.dot(rows, inward.reshape(inward.shape[0], -1), preferred_element_type=jnp.float32)
        half_width = projected.shape[1] // 2
        inner_act = (jax.nn.silu(projected[:, :half_width]) * projected[:, half_width:]).astype(jnp.bfloat16)
        return jnp.dot(inner_act, outward, preferred_element_type=jnp.float32).astype(jnp.bfloat16)
    results = lax.map(one_expert, (member.T, weight_in, weight_out))
    slot_index = jnp.take_along_axis(ranking, chosen, axis=1).astype(jnp.int32)
    return results[chosen, slot_index]

def layer(current, documents, chosen, attn_gain, query_gain, key_gain, ffn_gain, router, weight_in, weight_out):
    normed = rms_norm(current, attn_gain).astype(jnp.bfloat16)
    mixed = attention(normed, documents, query_gain, key_gain)
    residual = current.astype(jnp.float32) + mixed.astype(jnp.float32)
    moe_in = rms_norm(residual, ffn_gain).astype(jnp.bfloat16)
    logits = jnp.dot(moe_in, router, preferred_element_type=jnp.float32)
    chances = jax.nn.softmax(logits, axis=-1)
    picked = jnp.take_along_axis(chances, chosen, axis=1)
    gate_weights = picked / lax.optimization_barrier(jnp.sum(picked, axis=1, keepdims=True))
    outputs = expert_outputs(moe_in, chosen, weight_in, weight_out)
    combined = lax.optimization_barrier(jnp.sum(gate_weights[:, :, None] * outputs.astype(jnp.float32), axis=1))
    return (residual + combined).astype(jnp.bfloat16)

def reference(hidden_held, fresh_rows, doc_held, doc_fresh, routes, attn_gain, query_gain, key_gain, ffn_gain, router, weight_in, weight_out):
    currents = [hidden_held[layer_index] for layer_index in range(LAYERS)]
    documents = [doc_held[layer_index] for layer_index in range(LAYERS)]
    rows_out = []
    for step_index in range(TICKS):
        made = []
        for layer_index in range(LAYERS):
            made.append(layer(currents[layer_index], documents[layer_index], routes[step_index, layer_index], attn_gain[layer_index], query_gain[layer_index], key_gain[layer_index], ffn_gain[layer_index], router[layer_index], weight_in[layer_index], weight_out[layer_index]))
        rows_out.append(jnp.stack(made))
        if step_index + 1 < TICKS:
            currents = [fresh_rows[step_index]] + made[:-1]
            documents = [doc_fresh[step_index]] + documents[:-1]
    return jnp.stack(rows_out)
```

```python
import jax
import jax.numpy as jnp
import numpy as np
from jax import lax
from jax.experimental import pallas as pl
from jax.experimental.pallas import tpu as pltpu
from jax.sharding import PartitionSpec as P

MESH = pl.DeviceIdType.MESH
BF = jnp.bfloat16
F32 = jnp.float32
TOK = 128
D = 4096
HALF = 2048
CH = 512
NCH = HALF // CH
EXP = 32
CAP = 12
MSG = CAP * NCH
ROWS = EXP * MSG
QUAD = 4 * MSG
SLOTS = EXP * CAP
HID = 768
EPS = 1e-06


def _constants():
    row = np.arange(ROWS)
    chunk = (row % MSG) // CAP
    key = (row // MSG) * CAP + row % CAP + 1024 * chunk
    key_col = np.broadcast_to(key[:, None], (ROWS, TOK)).astype(np.float32)
    key_row = np.broadcast_to(key[None, :], (8, ROWS)).astype(np.float32)
    sort = np.zeros((QUAD, QUAD), np.float32)
    for j in range(4):
        for c in range(NCH):
            for slot in range(CAP):
                sort[c * 48 + j * CAP + slot, j * MSG + c * CAP + slot] = 1.0
    before = np.triu(np.ones((TOK, TOK), np.float32), 1)
    return key_col, key_row, sort, sort.T.copy(), before


def _kernel(
    held,
    fresh,
    ids_held,
    ids_fresh,
    routes,
    attn_gain,
    query_gain,
    key_gain,
    ffn_gain,
    router,
    w_in_hbm,
    w_out_hbm,
    key_col,
    key_row,
    sort,
    unsort,
    before,
    out_hbm,
    w_in,
    w_out,
    recv_d,
    recv_c,
    send_d,
    send_c,
    rows_in,
    inner,
    staged,
    pick,
    comb,
    cur,
    normed,
    prior,
    res,
    moe,
    carry,
    out_half,
    sums,
    stat_send,
    stat_recv,
    row_send,
    row_recv,
    ids_own,
    ids_pri,
    s_w,
    s_ids_send,
    s_ids_recv,
    s_prior_send,
    s_prior_recv,
    s_stat_send,
    s_stat_recv,
    s_carry,
    s_row_send,
    s_row_recv,
    s_d_send,
    s_d_recv,
    s_c_send,
    s_c_recv,
    s_out,
    s_out_recv,
):
    s = lax.axis_index("section")
    e = lax.axis_index("expert")
    h = lax.axis_index("dp")
    z, y, xl = e // 8, (e // 2) % 4, e % 2
    x = h * 2 + xl
    start_col = pl.multiple_of(h * HALF, HALF)

    def at(section, expert, dp):
        return {"section": section, "expert": expert, "dp": dp}

    def offset(j):
        k = (13 * j) % 32
        return k % 2, (k // 2) % 4, k // 8

    def ahead(m):
        dx, dy, dz = offset(m // 2)
        x2 = (x + dx + 2 * (m % 2)) % 4
        return ((z + dz) % 4) * 8 + ((y + dy) % 4) * 2 + x2 % 2, x2 // 2

    def behind(j):
        dx, dy, dz = offset(j)
        return ((z + 4 - dz) % 4) * 8 + ((y + 4 - dy) % 4) * 2 + (xl + dx) % 2

    nxt, prv = (e + 1) % EXP, (e + EXP - 1) % EXP

    load_in = pltpu.make_async_copy(w_in_hbm, w_in, s_w.at[0])
    load_out = pltpu.make_async_copy(w_out_hbm, w_out, s_w.at[1])
    load_in.start()
    load_out.start()

    barrier = pltpu.get_barrier_semaphore()

    @pl.loop(1, 2 * EXP)
    def _(m):
        e2, h2 = ahead(m)
        pl.semaphore_signal(barrier, inc=1, device_id=at(s, e2, h2), device_id_type=MESH)

    for e2, h2 in ((e, h), (e, 1 - h), (nxt, h), (prv, h)):
        pl.semaphore_signal(barrier, inc=1, device_id=at(1 - s, e2, h2), device_id_type=MESH)

    ids_own[0] = jnp.broadcast_to(ids_held[...], (8, TOK))

    @pl.when(s == 0)
    def _():
        ids_own[1] = jnp.broadcast_to(ids_fresh[...], (8, TOK))

    pl.semaphore_wait(barrier, 2 * EXP - 1 + 4)

    def send_ids(src, dst, i, j, device):
        return pltpu.make_async_remote_copy(
            src_ref=src,
            dst_ref=dst,
            send_sem=s_ids_send.at[i],
            recv_sem=s_ids_recv.at[j],
            device_id=device,
            device_id_type=MESH,
        )

    ids_0 = send_ids(ids_own.at[0], ids_pri.at[0], 0, 0, at(s, nxt, h))
    ids_1 = send_ids(ids_own.at[1], ids_pri.at[1], 1, 1, at(0, nxt, h))
    ids_2 = send_ids(ids_own.at[0], ids_own.at[1], 2, 2, at(1, e, h))
    ids_3 = send_ids(ids_own.at[0], ids_pri.at[1], 3, 1, at(1, nxt, h))
    ids_0.start()

    @pl.when(s == 0)
    def _():
        ids_1.start()
        ids_2.start()
        ids_3.start()

    def head_cols(c):
        return pl.ds(pl.multiple_of(c * TOK, TOK), TOK)

    def own_cols(c):
        return pl.ds(pl.multiple_of(start_col + c * TOK, TOK), TOK)

    def take_input(ref):
        sums[...] = jnp.zeros((TOK, TOK), F32)

        @pl.loop(0, D // TOK, unroll=8)
        def _(c):
            wide = ref[:, head_cols(c)].astype(F32)
            sums[...] += wide * wide

        cur[...] = ref[:, pl.ds(start_col, HALF)]

    @pl.loop(0, 2)
    def _(t):
        @pl.when(t == 0)
        def _():
            take_input(held)

        @pl.when((t == 1) & (s == 0))
        def _():
            take_input(fresh)

        @pl.when((t == 1) & (s == 1))
        def _():
            pltpu.make_async_remote_copy(
                src_ref=out_half.at[0],
                dst_ref=carry,
                send_sem=s_carry.at[0],
                recv_sem=s_carry.at[1],
                device_id=at(1, e, h),
                device_id_type=MESH,
            ).wait_recv()
            for i in range(2):
                pltpu.make_async_remote_copy(
                    src_ref=row_send,
                    dst_ref=row_recv.at[i],
                    send_sem=s_row_send.at[i],
                    recv_sem=s_row_recv.at[i],
                    device_id=at(1, e, h),
                    device_id_type=MESH,
                ).wait_recv()
            sums[...] = row_recv[0] + row_recv[1]
            cur[...] = carry[...]

        scale = lax.rsqrt(jnp.sum(sums[...], axis=1, keepdims=True) * (1.0 / D) + EPS)

        @pl.loop(0, HALF // TOK, unroll=4)
        def _(c):
            wide = cur[:, head_cols(c)].astype(F32)
            gain = attn_gain[:, own_cols(c)].astype(F32)
            normed[t, :, head_cols(c)] = (wide * scale * gain).astype(BF)

        send_prior = pltpu.make_async_remote_copy(
            src_ref=normed.at[t],
            dst_ref=prior.at[t],
            send_sem=s_prior_send.at[t],
            recv_sem=s_prior_recv.at[t],
            device_id=at(s, nxt, h),
            device_id_type=MESH,
        )
        send_prior.start()

        chosen = routes[t]
        label = lax.broadcasted_iota(jnp.int32, (EXP, TOK), 0)
        first = (label == chosen[0:1]).astype(F32)
        second = (label == chosen[1:2]).astype(F32)
        ranking = jnp.dot((first + second).astype(BF), before[...], preferred_element_type=F32)
        place_0 = jnp.sum((ranking + label.astype(F32) * CAP) * first, axis=0, keepdims=True)
        place_1 = jnp.sum((ranking + label.astype(F32) * CAP) * second, axis=0, keepdims=True)

        @pl.loop(0, ROWS // TOK)
        def _(r):
            rows = pl.ds(pl.multiple_of(r * TOK, TOK), TOK)
            keys = key_col[rows, :]
            for c in range(NCH):
                hit = (keys == place_0 + 1024.0 * c) | (keys == place_1 + 1024.0 * c)
                pick[rows, c * TOK : (c + 1) * TOK] = hit.astype(F32).astype(BF)

        @pl.when((t == 1) & (s == 1))
        def _():
            ids_2.wait_recv()

        @pl.when(t == 0)
        def _():
            ids_0.wait_recv()

        @pl.when(t == 1)
        def _():
            ids_1.wait_recv()

        row_ids = jnp.broadcast_to(ids_own[t, 0:1, :].astype(F32), (TOK, TOK))
        prior_ids = jnp.broadcast_to(ids_pri[t, 0:1, :].astype(F32), (TOK, TOK))
        col_ids = jnp.transpose(row_ids)
        causal = lax.broadcasted_iota(jnp.int32, (TOK, TOK), 1) <= lax.broadcasted_iota(
            jnp.int32, (TOK, TOK), 0
        )
        own_mask = jnp.where((col_ids == row_ids) & causal, 0.0, -1e30)
        pri_mask = jnp.where((col_ids == prior_ids) & (e > 0), 0.0, -1e30)
        send_prior.wait_recv()
        sums[...] = jnp.zeros((TOK, TOK), F32)

        @pl.loop(0, HALF // TOK // 4)
        def _(quad):
            for i in range(4):
                c = quad * 4 + i
                own = normed[t, :, head_cols(c)]
                pri = prior[t, :, head_cols(c)]
                q_gain = query_gain[:, own_cols(c)].astype(F32)
                k_gain = key_gain[:, own_cols(c)].astype(F32)
                queries = (own.astype(F32) * q_gain).astype(BF)
                own_keys = (own.astype(F32) * k_gain).astype(BF)
                pri_keys = (pri.astype(F32) * k_gain).astype(BF)
                dims = (((1,), (1,)), ((), ()))
                own_s = lax.dot_general(queries, own_keys, dims, preferred_element_type=F32)
                pri_s = lax.dot_general(queries, pri_keys, dims, preferred_element_type=F32)
                own_s = own_s * TOK**-0.5 + own_mask
                pri_s = pri_s * TOK**-0.5 + pri_mask
                top = jnp.max(jnp.maximum(own_s, pri_s), axis=1, keepdims=True)
                own_p = jnp.exp(own_s - top)
                pri_p = jnp.exp(pri_s - top)
                total = jnp.sum(own_p + pri_p, axis=1, keepdims=True)
                share = 1.0 / total
                mixed = jnp.dot((own_p * share).astype(BF), own, preferred_element_type=F32)
                mixed += jnp.dot((pri_p * share).astype(BF), pri, preferred_element_type=F32)
                summed = cur[:, head_cols(c)].astype(F32) + mixed.astype(BF).astype(F32)
                res[:, head_cols(c)] = summed
                sums[...] += summed * summed
                f_gain = ffn_gain[:, own_cols(c)].astype(F32)
                moe[:, head_cols(c)] = (summed * f_gain).astype(BF)

        stat_send[t, 0:TOK, :] = sums[...]
        stat_send[t, TOK:, :] = lax.dot_general(
            router[:, pl.ds(start_col, HALF)],
            moe[...],
            (((1,), (1,)), ((), ())),
            preferred_element_type=F32,
        )
        send_stat = pltpu.make_async_remote_copy(
            src_ref=stat_send.at[t],
            dst_ref=stat_recv.at[t],
            send_sem=s_stat_send.at[t],
            recv_sem=s_stat_recv.at[t],
            device_id=at(s, e, 1 - h),
            device_id_type=MESH,
        )
        send_stat.start()
        send_stat.wait_recv()
        sums[...] = stat_send[t, 0:TOK, :] + stat_recv[t, 0:TOK, :]
        logits = stat_send[t, TOK:, :] + stat_recv[t, TOK:, :]
        scale = lax.rsqrt(jnp.sum(sums[...], axis=1, keepdims=True) * (1.0 / D) + EPS)

        @pl.loop(0, HALF // TOK, unroll=4)
        def _(c):
            f_gain = ffn_gain[:, own_cols(c)].astype(F32)
            moe[:, head_cols(c)] = (res[:, head_cols(c)] * scale * f_gain).astype(BF)

        @pl.when(t == 1)
        def _():
            @pl.loop(1, 2 * EXP)
            def _(m):
                pltpu.make_async_remote_copy(
                    src_ref=send_d.at[pl.ds(0, MSG)],
                    dst_ref=recv_d.at[0, 0, 0, pl.ds(0, MSG)],
                    send_sem=s_d_send.at[m],
                    recv_sem=s_d_recv.at[0, 0],
                    device_id=at(s, nxt, h),
                    device_id_type=MESH,
                ).wait_send()

        @pl.loop(0, EXP // 4)
        def _(g):
            rows = pl.ds(pl.multiple_of(g * QUAD, QUAD), QUAD)
            total = jnp.zeros((QUAD, CH), F32)
            for c in range(NCH):
                total += jnp.dot(
                    pick[rows, c * TOK : (c + 1) * TOK],
                    moe[:, c * CH : (c + 1) * CH],
                    preferred_element_type=F32,
                )
            send_d[rows, :] = total.astype(BF)

        @pl.loop(1, 2 * EXP)
        def _(m):
            e2, h2 = ahead(m)
            j = m // 2
            pltpu.make_async_remote_copy(
                src_ref=send_d.at[pl.ds(pl.multiple_of(e2 * MSG, MSG), MSG)],
                dst_ref=recv_d.at[t, j // 4, h, pl.ds(pl.multiple_of((j % 4) * MSG, MSG), MSG)],
                send_sem=s_d_send.at[m],
                recv_sem=s_d_recv.at[t, j // 4],
                device_id=at(s, e2, h2),
                device_id_type=MESH,
            ).start()

        pltpu.make_async_copy(
            send_d.at[pl.ds(pl.multiple_of(e * MSG, MSG), MSG)],
            recv_d.at[t, 0, h, pl.ds(0, MSG)],
            s_d_recv.at[t, 0],
        ).start()

        scale_row = jnp.transpose(jnp.broadcast_to(scale, (TOK, TOK)))
        logits = logits * scale_row[0:EXP, :]
        logit_0 = jnp.sum(logits * first, axis=0, keepdims=True)
        logit_1 = jnp.sum(logits * second, axis=0, keepdims=True)
        top = jnp.maximum(logit_0, logit_1)
        raised_0, raised_1 = jnp.exp(logit_0 - top), jnp.exp(logit_1 - top)
        gate_0 = raised_0 / (raised_0 + raised_1)
        gate_1 = raised_1 / (raised_0 + raised_1)

        def column(row):
            return jnp.transpose(jnp.broadcast_to(row, (TOK, TOK)))

        gate_0, gate_1 = column(gate_0), column(gate_1)
        place_0, place_1 = column(place_0), column(place_1)

        @pl.loop(0, ROWS // TOK)
        def _(r):
            cols = pl.ds(pl.multiple_of(r * TOK, TOK), TOK)
            keys = key_row[0:1, cols]
            for c in range(NCH):
                value = jnp.where(keys == place_0 + 1024.0 * c, gate_0, 0.0)
                value += jnp.where(keys == place_1 + 1024.0 * c, gate_1, 0.0)
                comb[c, :, cols] = value.astype(BF)

        @pl.when(t == 0)
        def _():
            load_in.wait()
            load_out.wait()

        @pl.loop(0, EXP // 4)
        def _(g):
            pltpu.make_async_copy(
                recv_d.at[t, g], recv_d.at[t, g], s_d_recv.at[t, g]
            ).wait()
            for p in range(2):
                sorted_rows = jnp.dot(
                    sort[...], recv_d[t, g, p], preferred_element_type=F32
                ).astype(BF)
                for c in range(NCH):
                    rows_in[
                        pl.ds(pl.multiple_of(g * 48, 48), 48),
                        p * HALF + c * CH : p * HALF + (c + 1) * CH,
                    ] = sorted_rows[c * 48 : (c + 1) * 48]

        @pl.loop(0, HID // 256)
        def _(n):
            gate = jnp.dot(
                rows_in[...],
                w_in[:, pl.ds(pl.multiple_of(n * 256, 256), 256)],
                preferred_element_type=F32,
            )
            up = jnp.dot(
                rows_in[...],
                w_in[:, pl.ds(pl.multiple_of(HID + n * 256, 256), 256)],
                preferred_element_type=F32,
            )
            inner[:, pl.ds(pl.multiple_of(n * 256, 256), 256)] = (
                gate / (1.0 + jnp.exp(-gate)) * up
            ).astype(BF)

        @pl.when(t == 1)
        def _():
            @pl.loop(1, 2 * EXP)
            def _(m):
                pltpu.make_async_remote_copy(
                    src_ref=send_c.at[0, pl.ds(0, MSG)],
                    dst_ref=recv_c.at[0, 0, pl.ds(0, MSG)],
                    send_sem=s_c_send.at[m],
                    recv_sem=s_c_recv.at[0],
                    device_id=at(s, nxt, h),
                    device_id_type=MESH,
                ).wait_send()

        @pl.loop(0, 2)
        def _(p):
            for c in range(NCH):
                col = pl.multiple_of(p * HALF + c * CH, CH)
                staged[c] = jnp.dot(
                    inner[...], w_out[:, pl.ds(col, CH)], preferred_element_type=F32
                ).astype(BF)

            @pl.loop(0, EXP // 4)
            def _(g):
                rows = pl.ds(pl.multiple_of(g * 48, 48), 48)
                stack = staged[:, rows, :].reshape(QUAD, CH)
                packed = jnp.dot(unsort[...], stack, preferred_element_type=F32)
                send_c[p, pl.ds(pl.multiple_of(g * QUAD, QUAD), QUAD), :] = packed.astype(BF)

                @pl.loop(0, 4)
                def _(i):
                    j = g * 4 + i
                    remote = (j > 0) | (p != h)
                    src = send_c.at[p, pl.ds(pl.multiple_of(j * MSG, MSG), MSG)]
                    dst = recv_c.at[t, h, pl.ds(pl.multiple_of(e * MSG, MSG), MSG)]

                    @pl.when(remote)
                    def _():
                        m = jnp.where(j > 0, j * 2 + p, 1)
                        pltpu.make_async_remote_copy(
                            src_ref=src,
                            dst_ref=dst,
                            send_sem=s_c_send.at[m],
                            recv_sem=s_c_recv.at[t],
                            device_id=at(s, behind(j), p),
                            device_id_type=MESH,
                        ).start()

                    @pl.when(jnp.logical_not(remote))
                    def _():
                        pltpu.make_async_copy(src, dst, s_c_recv.at[t]).start()

        pltpu.make_async_copy(recv_c.at[t], recv_c.at[t], s_c_recv.at[t]).wait()
        sums[...] = jnp.zeros((TOK, TOK), F32)
        for c in range(NCH):
            combined = jnp.dot(comb[c], recv_c[t, 0], preferred_element_type=F32)
            combined += jnp.dot(comb[c], recv_c[t, 1], preferred_element_type=F32)
            final = (res[:, c * CH : (c + 1) * CH] + combined).astype(BF)
            out_half[t, :, c * CH : (c + 1) * CH] = final
            for i in range(CH // TOK):
                wide = final[:, i * TOK : (i + 1) * TOK].astype(F32)
                sums[...] += wide * wide

        @pl.when((t == 0) & (s == 0))
        def _():
            pltpu.make_async_remote_copy(
                src_ref=out_half.at[0],
                dst_ref=carry,
                send_sem=s_carry.at[0],
                recv_sem=s_carry.at[1],
                device_id=at(1, e, h),
                device_id_type=MESH,
            ).start()
            row_send[...] = sums[...]
            for i in range(2):
                pltpu.make_async_remote_copy(
                    src_ref=row_send,
                    dst_ref=row_recv.at[h],
                    send_sem=s_row_send.at[i],
                    recv_sem=s_row_recv.at[h],
                    device_id=at(1, e, (h + i) % 2),
                    device_id_type=MESH,
                ).start()

        half_out = out_hbm.at[t, :, pl.ds(start_col, HALF)]
        pltpu.make_async_copy(out_half.at[t], half_out, s_out.at[t, 0]).start()
        pltpu.make_async_remote_copy(
            src_ref=out_half.at[t],
            dst_ref=half_out,
            send_sem=s_out.at[t, 1],
            recv_sem=s_out_recv.at[t],
            device_id=at(s, e, 1 - h),
            device_id_type=MESH,
        ).start()

    @pl.loop(0, 2)
    def _(t):
        other_out = out_hbm.at[t, :, pl.ds(pl.multiple_of((1 - h) * HALF, HALF), HALF)]
        pltpu.make_async_copy(
            out_half.at[t], out_hbm.at[t, :, pl.ds(start_col, HALF)], s_out.at[t, 0]
        ).wait()
        done = pltpu.make_async_remote_copy(
            src_ref=out_half.at[t],
            dst_ref=other_out,
            send_sem=s_out.at[t, 1],
            recv_sem=s_out_recv.at[t],
            device_id=at(s, e, 1 - h),
            device_id_type=MESH,
        )
        done.wait_send()
        done.wait_recv()
        pltpu.make_async_remote_copy(
            src_ref=normed.at[t],
            dst_ref=prior.at[t],
            send_sem=s_prior_send.at[t],
            recv_sem=s_prior_recv.at[t],
            device_id=at(s, nxt, h),
            device_id_type=MESH,
        ).wait_send()
        pltpu.make_async_remote_copy(
            src_ref=stat_send.at[t],
            dst_ref=stat_recv.at[t],
            send_sem=s_stat_send.at[t],
            recv_sem=s_stat_recv.at[t],
            device_id=at(s, e, 1 - h),
            device_id_type=MESH,
        ).wait_send()

    @pl.loop(1, 2 * EXP)
    def _(m):
        pltpu.make_async_remote_copy(
            src_ref=send_d.at[pl.ds(0, MSG)],
            dst_ref=recv_d.at[0, 0, 0, pl.ds(0, MSG)],
            send_sem=s_d_send.at[m],
            recv_sem=s_d_recv.at[0, 0],
            device_id=at(s, nxt, h),
            device_id_type=MESH,
        ).wait_send()
        pltpu.make_async_remote_copy(
            src_ref=send_c.at[0, pl.ds(0, MSG)],
            dst_ref=recv_c.at[0, 0, pl.ds(0, MSG)],
            send_sem=s_c_send.at[m],
            recv_sem=s_c_recv.at[0],
            device_id=at(s, nxt, h),
            device_id_type=MESH,
        ).wait_send()

    ids_0.wait_send()

    @pl.when(s == 0)
    def _():
        ids_1.wait_send()
        ids_2.wait_send()
        ids_3.wait_send()
        pltpu.make_async_remote_copy(
            src_ref=out_half.at[0],
            dst_ref=carry,
            send_sem=s_carry.at[0],
            recv_sem=s_carry.at[1],
            device_id=at(1, e, h),
            device_id_type=MESH,
        ).wait_send()
        for i in range(2):
            pltpu.make_async_remote_copy(
                src_ref=row_send,
                dst_ref=row_recv.at[h],
                send_sem=s_row_send.at[i],
                recv_sem=s_row_recv.at[h],
                device_id=at(1, e, (h + i) % 2),
                device_id_type=MESH,
            ).wait_send()


def body(
    hidden_held,
    fresh_rows,
    doc_held,
    doc_fresh,
    routes,
    attn_gain,
    query_gain,
    key_gain,
    ffn_gain,
    router,
    weight_in,
    weight_out,
):
    key_col, key_row, sort, unsort, before = _constants()
    vmem = pl.BlockSpec(memory_space=pltpu.VMEM)
    hbm = pl.BlockSpec(memory_space=pl.ANY)
    dma = pltpu.SemaphoreType.DMA
    out = pl.pallas_call(
        _kernel,
        out_shape=jax.ShapeDtypeStruct((2, TOK, D), BF),
        in_specs=[vmem] * 10 + [hbm] * 2 + [vmem] * 5,
        out_specs=hbm,
        scratch_shapes=[
            pltpu.VMEM((D, 2 * HID), BF),
            pltpu.VMEM((HID, D), BF),
            pltpu.VMEM((2, EXP // 4, 2, QUAD, CH), BF),
            pltpu.VMEM((2, 2, ROWS, CH), BF),
            pltpu.VMEM((ROWS, CH), BF),
            pltpu.VMEM((2, ROWS, CH), BF),
            pltpu.VMEM((SLOTS, D), BF),
            pltpu.VMEM((SLOTS, HID), BF),
            pltpu.VMEM((NCH, SLOTS, CH), BF),
            pltpu.VMEM((ROWS, NCH * TOK), BF),
            pltpu.VMEM((NCH, TOK, ROWS), BF),
            pltpu.VMEM((TOK, HALF), BF),
            pltpu.VMEM((2, TOK, HALF), BF),
            pltpu.VMEM((2, TOK, HALF), BF),
            pltpu.VMEM((TOK, HALF), F32),
            pltpu.VMEM((TOK, HALF), BF),
            pltpu.VMEM((TOK, HALF), BF),
            pltpu.VMEM((2, TOK, HALF), BF),
            pltpu.VMEM((TOK, TOK), F32),
            pltpu.VMEM((2, TOK + EXP, TOK), F32),
            pltpu.VMEM((2, TOK + EXP, TOK), F32),
            pltpu.VMEM((TOK, TOK), F32),
            pltpu.VMEM((2, TOK, TOK), F32),
            pltpu.VMEM((2, 8, TOK), jnp.int32),
            pltpu.VMEM((2, 8, TOK), jnp.int32),
            dma((2,)),
            dma((4,)),
            dma((3,)),
            dma((2,)),
            dma((2,)),
            dma((2,)),
            dma((2,)),
            dma((2,)),
            dma((2,)),
            dma((2,)),
            dma((2 * EXP,)),
            dma((2, EXP // 4)),
            dma((2 * EXP,)),
            dma((2,)),
            dma((2, 2)),
            dma((2,)),
        ],
        compiler_params=pltpu.CompilerParams(
            collective_id=0, has_side_effects=True, vmem_limit_bytes=60 << 20
        ),
        cost_estimate=pl.CostEstimate(
            flops=25_000_000_000, bytes_accessed=25_000_000, transcendentals=5_000_000
        ),
    )(
        hidden_held[0],
        fresh_rows[0],
        doc_held,
        doc_fresh,
        jnp.swapaxes(routes[:, 0], 1, 2),
        attn_gain,
        query_gain,
        key_gain,
        ffn_gain,
        router[0].T,
        weight_in.reshape(D, 2 * HID),
        weight_out[0, 0],
        jnp.asarray(key_col),
        jnp.asarray(key_row),
        jnp.asarray(sort, BF),
        jnp.asarray(unsort, BF),
        jnp.asarray(before, BF),
    )
    return out[:, None]


def solution(mesh):
    in_specs = (
        P("section", "expert", None),
        P(None, "expert", None),
        P("section", "expert"),
        P(None, "expert"),
        P(None, "section", "expert", None),
        P("section", None),
        P("section", None),
        P("section", None),
        P("section", None),
        P("section", None, None),
        P("section", "expert", None, None, "dp"),
        P("section", "expert", "dp", None),
    )
    out_specs = P(None, "section", "expert", None)
    return jax.shard_map(body, mesh=mesh, in_specs=in_specs, out_specs=out_specs, check_vma=False)
```

```python
import jax
import jax.numpy as jnp
import numpy as np
from jax import lax
from jax.experimental import pallas as pl
from jax.experimental.pallas import tpu as pltpu
from jax.sharding import PartitionSpec as P

MESH = pl.DeviceIdType.MESH
BF = jnp.bfloat16
F32 = jnp.float32
TOK = 128
D = 4096
HALF = 2048
CH = 512
NCH = HALF // CH
EXP = 32
CAP = 12
MSG = CAP * NCH
ROWS = EXP * MSG
QUAD = 4 * MSG
SLOTS = EXP * CAP
HID = 768
WROWS = 256
EPS = 1e-06


def _constants():
    row = np.arange(ROWS)
    chunk = (row % MSG) // CAP
    key = (row // MSG) * CAP + row % CAP + 1024 * chunk
    key_col = np.broadcast_to(key[:, None], (ROWS, TOK)).astype(np.float32)
    key_row = np.broadcast_to(key[None, :], (8, ROWS)).astype(np.float32)
    sort = np.zeros((QUAD, QUAD), np.float32)
    for j in range(4):
        for c in range(NCH):
            for slot in range(CAP):
                sort[c * 48 + j * CAP + slot, j * MSG + c * CAP + slot] = 1.0
    before = np.triu(np.ones((TOK, TOK), np.float32), 1)
    return key_col, key_row, sort, sort.T.copy(), before


def _kernel(
    held,
    fresh,
    ids_held,
    ids_fresh,
    routes,
    attn_gain,
    query_gain,
    key_gain,
    ffn_gain,
    router,
    w_in_hbm,
    w_out_hbm,
    key_col,
    key_row,
    sort,
    unsort,
    before,
    out_hbm,
    w_part,
    w_in,
    w_out,
    recv_d,
    recv_c,
    send_d,
    send_c,
    rows_in,
    inner,
    staged,
    pick,
    comb,
    cur,
    normed,
    far,
    prior,
    res,
    moe,
    out_half,
    sums,
    stat_send,
    stat_recv,
    row_send,
    row_recv,
    columns,
    ids_own,
    ids_pri,
    s_w,
    s_ids_send,
    s_ids_recv,
    s_prior_send,
    s_prior_recv,
    s_stat_send,
    s_stat_recv,
    s_carry,
    s_row_send,
    s_row_recv,
    s_d_send,
    s_d_recv,
    s_c_send,
    s_c_recv,
    s_out,
    s_out_send,
    s_out_recv,
):
    s = lax.axis_index("section")
    e = lax.axis_index("expert")
    h = lax.axis_index("dp")
    z, y, xl = e // 8, (e // 2) % 4, e % 2
    x = h * 2 + xl
    start_col = pl.multiple_of(h * HALF, HALF)

    def at(section, expert, dp):
        return {"section": section, "expert": expert, "dp": dp}

    def offset(j):
        k = (13 * j) % 32
        return k % 2, (k // 2) % 4, k // 8

    def ahead(m):
        dx, dy, dz = offset(m // 2)
        x2 = (x + dx + 2 * (m % 2)) % 4
        return ((z + dz) % 4) * 8 + ((y + dy) % 4) * 2 + x2 % 2, x2 // 2

    def behind(j):
        dx, dy, dz = offset(j)
        return ((z + 4 - dz) % 4) * 8 + ((y + 4 - dy) % 4) * 2 + (xl + dx) % 2

    nxt, prv = (e + 1) % EXP, (e + EXP - 1) % EXP

    load_out = pltpu.make_async_copy(w_out_hbm, w_out, s_w.at[2])
    load_out.start()

    def load_in(i):
        return pltpu.make_async_copy(
            w_in_hbm.at[pl.ds(i * WROWS, WROWS)], w_part.at[i % 2], s_w.at[i % 2]
        )

    load_in(0).start()
    load_in(1).start()

    barrier = pltpu.get_barrier_semaphore()

    @pl.loop(1, 2 * EXP)
    def _(m):
        e2, h2 = ahead(m)
        pl.semaphore_signal(barrier, inc=1, device_id=at(s, e2, h2), device_id_type=MESH)

    for e2, h2 in ((e, h), (e, 1 - h), (nxt, h), (prv, h)):
        pl.semaphore_signal(barrier, inc=1, device_id=at(1 - s, e2, h2), device_id_type=MESH)

    ids_own[0] = jnp.broadcast_to(ids_held[...], (8, TOK))

    @pl.when(s == 0)
    def _():
        ids_own[1] = jnp.broadcast_to(ids_fresh[...], (8, TOK))

    def send_ids(src, dst, i, j, device):
        return pltpu.make_async_remote_copy(
            src_ref=src,
            dst_ref=dst,
            send_sem=s_ids_send.at[i],
            recv_sem=s_ids_recv.at[j],
            device_id=device,
            device_id_type=MESH,
        )

    ids_0 = send_ids(ids_own.at[0], ids_pri.at[0], 0, 0, at(s, nxt, h))
    ids_1 = send_ids(ids_own.at[1], ids_pri.at[1], 1, 1, at(0, nxt, h))
    ids_2 = send_ids(ids_own.at[0], ids_own.at[1], 2, 2, at(1, e, h))
    ids_3 = send_ids(ids_own.at[0], ids_pri.at[1], 3, 1, at(1, nxt, h))
    def head_cols(c):
        return pl.ds(pl.multiple_of(c * TOK, TOK), TOK)

    def own_cols(c):
        return pl.ds(pl.multiple_of(start_col + c * TOK, TOK), TOK)

    def take_input(ref, t):
        def add(i, total):
            for j in range(8):
                wide = ref[:, head_cols(i * 8 + j)].astype(F32)
                total = total + wide * wide
            return total

        total = lax.fori_loop(0, D // TOK // 8, add, jnp.zeros((TOK, TOK), F32))
        scale = lax.rsqrt(jnp.sum(total, axis=1, keepdims=True) * (1.0 / D) + EPS)
        cur[t] = ref[:, pl.ds(start_col, HALF)]
        far_col = pl.multiple_of((1 - h) * HALF + HALF // 2, HALF // 2)

        @pl.loop(0, 2)
        def _(i):
            for j in range(4):
                c = i * 4 + j
                cols = pl.ds(pl.multiple_of(far_col + c * TOK, TOK), TOK)
                wide = ref[:, cols].astype(F32)
                gain = attn_gain[:, cols].astype(F32)
                far[t, :, head_cols(c)] = (wide * scale * gain).astype(BF)

        norm(t, scale)
        prior_copy(t, 0, 0).start()
        prior_copy(t, 1, 1).start()

    def norm(t, scale):
        @pl.loop(0, HALF // TOK, unroll=4)
        def _(c):
            wide = cur[t, :, head_cols(c)].astype(F32)
            gain = attn_gain[:, own_cols(c)].astype(F32)
            normed[t, :, head_cols(c)] = (wide * scale * gain).astype(BF)

    def prior_copy(t, piece, across):
        cols = pl.ds(piece * (HALF // 2), HALF // 2)
        return pltpu.make_async_remote_copy(
            src_ref=far.at[t] if across else normed.at[t, :, cols],
            dst_ref=prior.at[t, :, cols],
            send_sem=s_prior_send.at[t, piece],
            recv_sem=s_prior_recv.at[t, piece],
            device_id=at(s, nxt, 1 - h if across else h),
            device_id_type=MESH,
        )

    def carry_copy():
        return pltpu.make_async_remote_copy(
            src_ref=out_half.at[0],
            dst_ref=cur.at[1],
            send_sem=s_carry.at[0],
            recv_sem=s_carry.at[1],
            device_id=at(1, e, h),
            device_id_type=MESH,
        )

    def row_copy(i):
        return pltpu.make_async_remote_copy(
            src_ref=row_send,
            dst_ref=row_recv.at[h],
            send_sem=s_row_send.at[i],
            recv_sem=s_row_recv.at[h],
            device_id=at(1, e, (h + i) % 2),
            device_id_type=MESH,
        )

    def stat_copy(t):
        return pltpu.make_async_remote_copy(
            src_ref=stat_send.at[t],
            dst_ref=stat_recv.at[t],
            send_sem=s_stat_send.at[t],
            recv_sem=s_stat_recv.at[t],
            device_id=at(s, e, 1 - h),
            device_id_type=MESH,
        )

    pl.semaphore_wait(barrier, 2 * EXP - 1 + 4)
    take_input(held, 0)
    ids_0.start()

    @pl.when(s == 0)
    def _():
        ids_1.start()
        ids_2.start()
        ids_3.start()
        take_input(fresh, 1)

    def send_dispatch(t):
        @pl.loop(1, 2 * EXP)
        def _(m):
            e2, h2 = ahead(m)
            j = m // 2
            pltpu.make_async_remote_copy(
                src_ref=send_d.at[t, pl.ds(pl.multiple_of(e2 * MSG, MSG), MSG)],
                dst_ref=recv_d.at[t, j // 4, h, pl.ds(pl.multiple_of((j % 4) * MSG, MSG), MSG)],
                send_sem=s_d_send.at[t, m],
                recv_sem=s_d_recv.at[t, j // 4],
                device_id=at(s, e2, h2),
                device_id_type=MESH,
            ).start()

        pltpu.make_async_copy(
            send_d.at[t, pl.ds(pl.multiple_of(e * MSG, MSG), MSG)],
            recv_d.at[t, 0, h, pl.ds(0, MSG)],
            s_d_recv.at[t, 0],
        ).start()
    def attention_stage(t):
        @pl.when((t == 1) & (s == 1))
        def _():
            carry_copy().wait_recv()
            for i in range(2):
                pltpu.make_async_remote_copy(
                    src_ref=row_send,
                    dst_ref=row_recv.at[i],
                    send_sem=s_row_send.at[i],
                    recv_sem=s_row_recv.at[i],
                    device_id=at(1, e, h),
                    device_id_type=MESH,
                ).wait_recv()
            total = row_recv[0] + row_recv[1]
            norm(1, lax.rsqrt(jnp.sum(total, axis=1, keepdims=True) * (1.0 / D) + EPS))
            prior_copy(1, 0, 0).start()
            prior_copy(1, 1, 0).start()
            ids_2.wait_recv()

        chosen = routes[t]
        label = lax.broadcasted_iota(jnp.int32, (EXP, TOK), 0)
        first = (label == chosen[0:1]).astype(F32)
        second = (label == chosen[1:2]).astype(F32)
        ranking = jnp.dot((first + second).astype(BF), before[...], preferred_element_type=F32)
        place_0 = jnp.sum((ranking + label.astype(F32) * CAP) * first, axis=0, keepdims=True)
        place_1 = jnp.sum((ranking + label.astype(F32) * CAP) * second, axis=0, keepdims=True)

        @pl.loop(0, ROWS // TOK)
        def _(r):
            rows = pl.ds(pl.multiple_of(r * TOK, TOK), TOK)
            keys = key_col[rows, :]
            for c in range(NCH):
                hit = (keys == place_0 + 1024.0 * c) | (keys == place_1 + 1024.0 * c)
                pick[rows, c * TOK : (c + 1) * TOK] = hit.astype(F32).astype(BF)

        @pl.when(t == 0)
        def _():
            ids_0.wait_recv()

        @pl.when(t == 1)
        def _():
            ids_1.wait_recv()

        row_ids = jnp.broadcast_to(ids_own[t, 0:1, :].astype(F32), (TOK, TOK))
        prior_ids = jnp.broadcast_to(ids_pri[t, 0:1, :].astype(F32), (TOK, TOK))
        col_ids = jnp.transpose(row_ids)
        causal = lax.broadcasted_iota(jnp.int32, (TOK, TOK), 1) <= lax.broadcasted_iota(
            jnp.int32, (TOK, TOK), 0
        )
        own_mask = jnp.where((col_ids == row_ids) & causal, 0.0, -1e30)
        pri_mask = jnp.where((col_ids == prior_ids) & (e > 0), 0.0, -1e30)
        sums[...] = jnp.zeros((TOK, TOK), F32)

        @pl.loop(0, NCH)
        def _(quad):
            @pl.when(quad == 0)
            def _():
                prior_copy(t, 0, 0).wait_recv()

            @pl.when(quad == 2)
            def _():
                prior_copy(t, 1, 0).wait_recv()

            rows = pl.ds(pl.multiple_of(quad * TOK, TOK), TOK)
            for i in range(4):
                c = quad * 4 + i
                own = normed[t, :, head_cols(c)]
                pri = prior[t, :, head_cols(c)]
                q_gain = query_gain[:, own_cols(c)].astype(F32)
                k_gain = key_gain[:, own_cols(c)].astype(F32)
                queries = (own.astype(F32) * q_gain).astype(BF)
                own_keys = (own.astype(F32) * k_gain).astype(BF)
                pri_keys = (pri.astype(F32) * k_gain).astype(BF)
                dims = (((1,), (1,)), ((), ()))
                own_s = lax.dot_general(queries, own_keys, dims, preferred_element_type=F32)
                pri_s = lax.dot_general(queries, pri_keys, dims, preferred_element_type=F32)
                own_s = own_s * TOK**-0.5 + own_mask
                pri_s = pri_s * TOK**-0.5 + pri_mask
                top = jnp.max(jnp.maximum(own_s, pri_s), axis=1, keepdims=True)
                own_p = jnp.exp(own_s - top)
                pri_p = jnp.exp(pri_s - top)
                total = jnp.sum(own_p + pri_p, axis=1, keepdims=True)
                share = 1.0 / total
                mixed = jnp.dot((own_p * share).astype(BF), own, preferred_element_type=F32)
                mixed += jnp.dot((pri_p * share).astype(BF), pri, preferred_element_type=F32)
                summed = cur[t, :, head_cols(c)].astype(F32) + mixed.astype(BF).astype(F32)
                res[t, :, head_cols(c)] = summed
                sums[...] += summed * summed
                f_gain = ffn_gain[:, own_cols(c)].astype(F32)
                moe[rows, i * TOK : (i + 1) * TOK] = (summed * f_gain).astype(BF)

        stat_send[t, 0:TOK, :] = sums[...]
        part = jnp.zeros((EXP, TOK), F32)
        for c in range(NCH):
            part += lax.dot_general(
                router[:, pl.ds(pl.multiple_of(start_col + c * CH, CH), CH)],
                moe[c * TOK : (c + 1) * TOK, :],
                (((1,), (1,)), ((), ())),
                preferred_element_type=F32,
            )
        stat_send[t, TOK:, :] = part
        stat_copy(t).start()
        stat_copy(t).wait_recv()
        sums[...] = stat_send[t, 0:TOK, :] + stat_recv[t, 0:TOK, :]
        logits = stat_send[t, TOK:, :] + stat_recv[t, TOK:, :]
        scale = lax.rsqrt(jnp.sum(sums[...], axis=1, keepdims=True) * (1.0 / D) + EPS)

        @pl.loop(0, NCH)
        def _(quad):
            rows = pl.ds(pl.multiple_of(quad * TOK, TOK), TOK)
            for i in range(4):
                c = quad * 4 + i
                f_gain = ffn_gain[:, own_cols(c)].astype(F32)
                moe[rows, i * TOK : (i + 1) * TOK] = (
                    res[t, :, head_cols(c)] * scale * f_gain
                ).astype(BF)

        @pl.loop(0, EXP // 4)
        def _(g):
            rows = pl.ds(pl.multiple_of(g * QUAD, QUAD), QUAD)
            send_d[t, rows, :] = jnp.dot(
                pick[rows, :], moe[...], preferred_element_type=F32
            ).astype(BF)

        send_dispatch(t)

        scale_row = jnp.transpose(jnp.broadcast_to(scale, (TOK, TOK)))
        logits = logits * scale_row[0:EXP, :]
        logit_0 = jnp.sum(logits * first, axis=0, keepdims=True)
        logit_1 = jnp.sum(logits * second, axis=0, keepdims=True)
        top = jnp.maximum(logit_0, logit_1)
        raised_0, raised_1 = jnp.exp(logit_0 - top), jnp.exp(logit_1 - top)

        def column(row):
            return jnp.transpose(jnp.broadcast_to(row, (TOK, TOK)))

        columns[t, 0] = column(raised_0 / (raised_0 + raised_1))
        columns[t, 1] = column(raised_1 / (raised_0 + raised_1))
        columns[t, 2] = column(place_0)
        columns[t, 3] = column(place_1)

        @pl.when(t == 0)
        def _():
            @pl.loop(0, D // WROWS)
            def _(i):
                load_in(i).wait()
                rows = pl.ds(pl.multiple_of(i * WROWS, WROWS), WROWS)
                w_in[rows, :] = w_part[i % 2].reshape(WROWS, 2 * HID)

                @pl.when(i + 2 < D // WROWS)
                def _():
                    load_in(i + 2).start()

            load_out.wait()

    def expert_stage(t):
        @pl.loop(0, 2)
        def _(block):
            @pl.loop(0, 4)
            def _(i):
                g = block * 4 + i
                pltpu.make_async_copy(
                    recv_d.at[t, g], recv_d.at[t, g], s_d_recv.at[t, g]
                ).wait()
                for p in range(2):
                    sorted_rows = jnp.dot(
                        sort[...], recv_d[t, g, p], preferred_element_type=F32
                    ).astype(BF)
                    for c in range(NCH):
                        rows_in[
                            pl.ds(pl.multiple_of(i * 48, 48), 48),
                            p * HALF + c * CH : p * HALF + (c + 1) * CH,
                        ] = sorted_rows[c * 48 : (c + 1) * 48]

            @pl.loop(0, HID // 256)
            def _(n):
                gate = jnp.dot(
                    rows_in[...],
                    w_in[:, pl.ds(pl.multiple_of(n * 256, 256), 256)],
                    preferred_element_type=F32,
                )
                up = jnp.dot(
                    rows_in[...],
                    w_in[:, pl.ds(pl.multiple_of(HID + n * 256, 256), 256)],
                    preferred_element_type=F32,
                )
                inner[:, pl.ds(pl.multiple_of(n * 256, 256), 256)] = (
                    gate / (1.0 + jnp.exp(-gate)) * up
                ).astype(BF)

            @pl.loop(0, 2)
            def _(p):
                for c in range(NCH):
                    col = pl.multiple_of(p * HALF + c * CH, CH)
                    staged[c] = jnp.dot(
                        inner[...], w_out[:, pl.ds(col, CH)], preferred_element_type=F32
                    ).astype(BF)

                @pl.loop(0, 4)
                def _(i):
                    g = block * 4 + i
                    rows = pl.ds(pl.multiple_of(i * 48, 48), 48)
                    stack = staged[:, rows, :].reshape(QUAD, CH)
                    packed = jnp.dot(unsort[...], stack, preferred_element_type=F32)
                    send_c[t, p, pl.ds(pl.multiple_of(g * QUAD, QUAD), QUAD), :] = packed.astype(BF)

                    @pl.when((s == 1) | (t == 0))
                    def _():
                        send_results(t, p, g)

    def send_results(t, p, g):
        @pl.loop(0, 4)
        def _(i):
            j = g * 4 + i
            remote = (j > 0) | (p != h)
            src = send_c.at[t, p, pl.ds(pl.multiple_of(j * MSG, MSG), MSG)]
            dst = recv_c.at[t, h, pl.ds(pl.multiple_of(e * MSG, MSG), MSG)]

            @pl.when(remote)
            def _():
                m = jnp.where(j > 0, j * 2 + p, 1)
                pltpu.make_async_remote_copy(
                    src_ref=src,
                    dst_ref=dst,
                    send_sem=s_c_send.at[t, m],
                    recv_sem=s_c_recv.at[t],
                    device_id=at(s, behind(j), p),
                    device_id_type=MESH,
                ).start()

            @pl.when(jnp.logical_not(remote))
            def _():
                pltpu.make_async_copy(src, dst, s_c_recv.at[t]).start()

    def combine_stage(t):
        @pl.loop(0, ROWS // TOK)
        def _(r):
            cols = pl.ds(pl.multiple_of(r * TOK, TOK), TOK)
            keys = key_row[0:1, cols]
            for c in range(NCH):
                value = jnp.where(keys == columns[t, 2] + 1024.0 * c, columns[t, 0], 0.0)
                value += jnp.where(keys == columns[t, 3] + 1024.0 * c, columns[t, 1], 0.0)
                comb[c, :, cols] = value.astype(BF)

        pltpu.make_async_copy(recv_c.at[t], recv_c.at[t], s_c_recv.at[t]).wait()
        total = jnp.zeros((TOK, TOK), F32)
        for c in range(NCH):
            combined = jnp.dot(comb[c], recv_c[t, 0], preferred_element_type=F32)
            combined += jnp.dot(comb[c], recv_c[t, 1], preferred_element_type=F32)
            final = (res[t, :, c * CH : (c + 1) * CH] + combined).astype(BF)
            out_half[t, :, c * CH : (c + 1) * CH] = final
            for i in range(CH // TOK):
                wide = final[:, i * TOK : (i + 1) * TOK].astype(F32)
                total = total + wide * wide

            @pl.when(t == 1)
            def _():
                far_out(1, c).start()

        @pl.when((t == 0) & (s == 0))
        def _():
            carry_copy().start()
            row_send[...] = total
            for i in range(2):
                row_copy(i).start()

            @pl.loop(0, 2)
            def _(p):
                @pl.loop(0, EXP // 4)
                def _(g):
                    send_results(1, p, g)

        @pl.when(t == 0)
        def _():
            for c in range(NCH):
                far_out(0, c).start()

        near_out(t).start()

    def near_out(t):
        return pltpu.make_async_copy(
            out_half.at[t], out_hbm.at[t, :, pl.ds(start_col, HALF)], s_out.at[t]
        )

    def far_out(t, c):
        return pltpu.make_async_remote_copy(
            src_ref=out_half.at[t, :, pl.ds(c * CH, CH)],
            dst_ref=out_hbm.at[t, :, pl.ds(pl.multiple_of(start_col + c * CH, CH), CH)],
            send_sem=s_out_send.at[t, c],
            recv_sem=s_out_recv.at[t, c],
            device_id=at(s, e, 1 - h),
            device_id_type=MESH,
        )

    @pl.loop(0, 6)
    def _(step):
        @pl.when((step == 0) | (step == 1 + s))
        def _():
            attention_stage((step + 1) // 2)

        @pl.when((step == 2 - s) | (step == 3 + s))
        def _():
            expert_stage(step // 3)

        @pl.when((step == 4 - s) | (step == 5))
        def _():
            combine_stage(step // 5)

    @pl.loop(0, 2)
    def _(t):
        near_out(t).wait()
        for c in range(NCH):
            far_out(t, c).wait()
        prior_copy(t, 0, 0).wait_send()
        prior_copy(t, 1, 0).wait_send()
        stat_copy(t).wait_send()

    @pl.loop(1, 2 * EXP)
    def _(m):
        for t in range(2):
            pltpu.make_async_remote_copy(
                src_ref=send_c.at[0, 0, pl.ds(0, MSG)],
                dst_ref=recv_c.at[0, 0, pl.ds(0, MSG)],
                send_sem=s_c_send.at[t, m],
                recv_sem=s_c_recv.at[0],
                device_id=at(s, nxt, h),
                device_id_type=MESH,
            ).wait_send()
            pltpu.make_async_remote_copy(
                src_ref=send_d.at[0, pl.ds(0, MSG)],
                dst_ref=recv_d.at[0, 0, 0, pl.ds(0, MSG)],
                send_sem=s_d_send.at[t, m],
                recv_sem=s_d_recv.at[0, 0],
                device_id=at(s, nxt, h),
                device_id_type=MESH,
            ).wait_send()

    ids_0.wait_send()

    @pl.when(s == 0)
    def _():
        ids_1.wait_send()
        ids_2.wait_send()
        ids_3.wait_send()
        carry_copy().wait_send()
        for i in range(2):
            row_copy(i).wait_send()


def body(
    hidden_held,
    fresh_rows,
    doc_held,
    doc_fresh,
    routes,
    attn_gain,
    query_gain,
    key_gain,
    ffn_gain,
    router,
    weight_in,
    weight_out,
):
    key_col, key_row, sort, unsort, before = _constants()
    vmem = pl.BlockSpec(memory_space=pltpu.VMEM)
    hbm = pl.BlockSpec(memory_space=pl.ANY)
    dma = pltpu.SemaphoreType.DMA
    out = pl.pallas_call(
        _kernel,
        out_shape=jax.ShapeDtypeStruct((2, TOK, D), BF),
        in_specs=[vmem] * 10 + [hbm] * 2 + [vmem] * 5,
        out_specs=hbm,
        scratch_shapes=[
            pltpu.VMEM((2, WROWS, 2, HID), BF),
            pltpu.VMEM((D, 2 * HID), BF),
            pltpu.VMEM((HID, D), BF),
            pltpu.VMEM((2, EXP // 4, 2, QUAD, CH), BF),
            pltpu.VMEM((2, 2, ROWS, CH), BF),
            pltpu.VMEM((2, ROWS, CH), BF),
            pltpu.VMEM((2, 2, ROWS, CH), BF),
            pltpu.VMEM((SLOTS // 2, D), BF),
            pltpu.VMEM((SLOTS // 2, HID), BF),
            pltpu.VMEM((NCH, SLOTS // 2, CH), BF),
            pltpu.VMEM((ROWS, NCH * TOK), BF),
            pltpu.VMEM((NCH, TOK, ROWS), BF),
            pltpu.VMEM((2, TOK, HALF), BF),
            pltpu.VMEM((2, TOK, HALF), BF),
            pltpu.VMEM((2, TOK, HALF // 2), BF),
            pltpu.VMEM((2, TOK, HALF), BF),
            pltpu.VMEM((2, TOK, HALF), F32),
            pltpu.VMEM((NCH * TOK, CH), BF),
            pltpu.VMEM((2, TOK, HALF), BF),
            pltpu.VMEM((TOK, TOK), F32),
            pltpu.VMEM((2, TOK + EXP, TOK), F32),
            pltpu.VMEM((2, TOK + EXP, TOK), F32),
            pltpu.VMEM((TOK, TOK), F32),
            pltpu.VMEM((2, TOK, TOK), F32),
            pltpu.VMEM((2, 4, TOK, TOK), F32),
            pltpu.VMEM((2, 8, TOK), jnp.int32),
            pltpu.VMEM((2, 8, TOK), jnp.int32),
            dma((3,)),
            dma((4,)),
            dma((3,)),
            dma((2, 2)),
            dma((2, 2)),
            dma((2,)),
            dma((2,)),
            dma((2,)),
            dma((2,)),
            dma((2,)),
            dma((2, 2 * EXP)),
            dma((2, EXP // 4)),
            dma((2, 2 * EXP)),
            dma((2,)),
            dma((2,)),
            dma((2, NCH)),
            dma((2, NCH)),
        ],
        compiler_params=pltpu.CompilerParams(
            collective_id=0, has_side_effects=True, vmem_limit_bytes=62 << 20
        ),
        cost_estimate=pl.CostEstimate(
            flops=25_000_000_000, bytes_accessed=25_000_000, transcendentals=5_000_000
        ),
    )(
        hidden_held[0],
        fresh_rows[0],
        doc_held,
        doc_fresh,
        jnp.swapaxes(routes[:, 0], 1, 2),
        attn_gain,
        query_gain,
        key_gain,
        ffn_gain,
        router[0].T,
        weight_in[0, 0],
        weight_out[0, 0],
        jnp.asarray(key_col),
        jnp.asarray(key_row),
        jnp.asarray(sort, BF),
        jnp.asarray(unsort, BF),
        jnp.asarray(before, BF),
    )
    return out[:, None]


def solution(mesh):
    in_specs = (
        P("section", "expert", None),
        P(None, "expert", None),
        P("section", "expert"),
        P(None, "expert"),
        P(None, "section", "expert", None),
        P("section", None),
        P("section", None),
        P("section", None),
        P("section", None),
        P("section", None, None),
        P("section", "expert", None, None, "dp"),
        P("section", "expert", "dp", None),
    )
    out_specs = P(None, "section", "expert", None)
    return jax.shard_map(body, mesh=mesh, in_specs=in_specs, out_specs=out_specs, check_vma=False)
```

```python
import jax
import jax.numpy as jnp
import numpy as np
from jax import lax
from jax.experimental import pallas as pl
from jax.experimental.pallas import tpu as pltpu
from jax.sharding import PartitionSpec as P

MESH = pl.DeviceIdType.MESH
BF = jnp.bfloat16
F32 = jnp.float32
TOK = 128
D = 4096
HALF = 2048
CH = 512
NCH = HALF // CH
EXP = 32
CAP = 12
MSG = CAP * NCH
ROWS = EXP * MSG
QUAD = 4 * MSG
SLOTS = EXP * CAP
HID = 768
WROWS = 256
EPS = 1e-06


def _constants():
    row = np.arange(ROWS)
    chunk = (row % MSG) // CAP
    key = (row // MSG) * CAP + row % CAP + 1024 * chunk
    key_col = np.broadcast_to(key[:, None], (ROWS, TOK)).astype(np.float32)
    key_row = np.broadcast_to(key[None, :], (8, ROWS)).astype(np.float32)
    sort = np.zeros((QUAD, QUAD), np.float32)
    for j in range(4):
        for c in range(NCH):
            for slot in range(CAP):
                sort[c * 48 + j * CAP + slot, j * MSG + c * CAP + slot] = 1.0
    before = np.triu(np.ones((TOK, TOK), np.float32), 1)
    return key_col, key_row, sort, sort.T.copy(), before


def _kernel(
    held_hbm,
    fresh_hbm,
    ids_held,
    ids_fresh,
    routes,
    attn_gain,
    query_gain,
    key_gain,
    ffn_gain,
    router,
    w_in_hbm,
    w_out_hbm,
    key_col_hbm,
    key_row,
    sort,
    unsort,
    before,
    out_hbm,
    held,
    fresh,
    key_col,
    w_part,
    w_in,
    w_out,
    recv_d,
    recv_c,
    send_d,
    send_c,
    rows_in,
    inner,
    staged,
    pick,
    comb,
    cur,
    normed,
    far,
    prior,
    res,
    moe,
    out_half,
    sums,
    stat_send,
    stat_recv,
    row_send,
    row_recv,
    columns,
    ids_own,
    ids_pri,
    s_w,
    s_in,
    s_ids_send,
    s_ids_recv,
    s_prior_send,
    s_prior_recv,
    s_stat_send,
    s_stat_recv,
    s_carry,
    s_row_send,
    s_row_recv,
    s_d_send,
    s_d_recv,
    s_c_send,
    s_c_recv,
    s_out,
    s_out_send,
    s_out_recv,
    s_here,
):
    s = lax.axis_index("section")
    e = lax.axis_index("expert")
    h = lax.axis_index("dp")
    z, y, xl = e // 8, (e // 2) % 4, e % 2
    x = h * 2 + xl
    start_col = pl.multiple_of(h * HALF, HALF)

    def at(section, expert, dp):
        return {"section": section, "expert": expert, "dp": dp}

    def offset(j):
        k = (13 * j) % 32
        return k % 2, (k // 2) % 4, k // 8

    def ahead(m):
        dx, dy, dz = offset(m // 2)
        x2 = (x + dx + 2 * (m % 2)) % 4
        return ((z + dz) % 4) * 8 + ((y + dy) % 4) * 2 + x2 % 2, x2 // 2

    def behind(j):
        dx, dy, dz = offset(j)
        return ((z + 4 - dz) % 4) * 8 + ((y + 4 - dy) % 4) * 2 + (xl + dx) % 2

    nxt, prv = (e + 1) % EXP, (e + EXP - 1) % EXP

    load_held = pltpu.make_async_copy(held_hbm, held, s_in.at[0])
    load_fresh = pltpu.make_async_copy(fresh_hbm, fresh, s_in.at[1])
    load_keys = pltpu.make_async_copy(key_col_hbm, key_col, s_in.at[2])
    load_held.start()
    barrier = pltpu.get_barrier_semaphore()

    def along(axis, i):
        if axis == 0:
            x2 = (x + i) % 4
            return at(s, e - xl + x2 % 2, x2 // 2)
        if axis == 1:
            return at(s, z * 8 + ((y + i) % 4) * 2 + xl, h)
        return at(s, ((z + i) % 4) * 8 + y * 2 + xl, h)

    def greet(axis, sem):
        for i in range(1, 4):
            pl.semaphore_signal(sem, inc=1, device_id=along(axis, i), device_id_type=MESH)

    for e2 in (nxt, prv):
        for h2 in (h, 1 - h):
            pl.semaphore_signal(barrier, inc=1, device_id=at(s, e2, h2), device_id_type=MESH)
    for e2, h2 in ((e, h), (e, 1 - h), (nxt, h), (prv, h)):
        pl.semaphore_signal(barrier, inc=1, device_id=at(1 - s, e2, h2), device_id_type=MESH)
    for axis in range(3):
        greet(axis, barrier)

    load_keys.start()
    load_fresh.start()
    load_out = pltpu.make_async_copy(w_out_hbm, w_out, s_w.at[2])
    load_out.start()

    def load_in(i):
        return pltpu.make_async_copy(
            w_in_hbm.at[pl.ds(i * WROWS, WROWS)], w_part.at[i % 2], s_w.at[i % 2]
        )

    load_in(0).start()
    load_in(1).start()

    ids_own[0] = jnp.broadcast_to(ids_held[...], (8, TOK))

    @pl.when(s == 0)
    def _():
        ids_own[1] = jnp.broadcast_to(ids_fresh[...], (8, TOK))

    def send_ids(src, dst, i, j, device):
        return pltpu.make_async_remote_copy(
            src_ref=src,
            dst_ref=dst,
            send_sem=s_ids_send.at[i],
            recv_sem=s_ids_recv.at[j],
            device_id=device,
            device_id_type=MESH,
        )

    ids_0 = send_ids(ids_own.at[0], ids_pri.at[0], 0, 0, at(s, nxt, h))
    ids_1 = send_ids(ids_own.at[1], ids_pri.at[1], 1, 1, at(0, nxt, h))
    ids_2 = send_ids(ids_own.at[0], ids_own.at[1], 2, 2, at(1, e, h))
    ids_3 = send_ids(ids_own.at[0], ids_pri.at[1], 3, 1, at(1, nxt, h))
    def head_cols(c):
        return pl.ds(pl.multiple_of(c * TOK, TOK), TOK)

    def own_cols(c):
        return pl.ds(pl.multiple_of(start_col + c * TOK, TOK), TOK)

    def take_input(ref, t):
        def add(i, total):
            for j in range(8):
                wide = ref[:, head_cols(i * 8 + j)].astype(F32)
                total = total + wide * wide
            return total

        total = lax.fori_loop(0, D // TOK // 8, add, jnp.zeros((TOK, TOK), F32))
        scale = lax.rsqrt(jnp.sum(total, axis=1, keepdims=True) * (1.0 / D) + EPS)
        cur[t] = ref[:, pl.ds(start_col, HALF)]
        far_col = pl.multiple_of((1 - h) * HALF + HALF // 2, HALF // 2)

        norm(t, scale, 2)
        for piece in range(2):
            for j in range(4):
                c = piece * 4 + j
                cols = pl.ds(pl.multiple_of(far_col + c * TOK, TOK), TOK)
                wide = ref[:, cols].astype(F32)
                gain = attn_gain[:, cols].astype(F32)
                far[t, :, head_cols(c)] = (wide * scale * gain).astype(BF)
            prior_copy(t, 2 + piece, 1).start()

    def norm(t, scale, sent):
        for piece in range(NCH):
            for i in range(4):
                c = piece * 4 + i
                wide = cur[t, :, head_cols(c)].astype(F32)
                gain = attn_gain[:, own_cols(c)].astype(F32)
                normed[t, :, head_cols(c)] = (wide * scale * gain).astype(BF)
            if piece < sent:
                prior_copy(t, piece, 0).start()

    def prior_copy(t, piece, across):
        cols = pl.ds(piece * CH, CH)
        return pltpu.make_async_remote_copy(
            src_ref=far.at[t, :, pl.ds(piece * CH - HALF // 2, CH)]
            if across
            else normed.at[t, :, cols],
            dst_ref=prior.at[t, :, cols],
            send_sem=s_prior_send.at[t, piece],
            recv_sem=s_prior_recv.at[t, piece],
            device_id=at(s, nxt, 1 - h if across else h),
            device_id_type=MESH,
        )

    def carry_copy():
        return pltpu.make_async_remote_copy(
            src_ref=out_half.at[0],
            dst_ref=cur.at[1],
            send_sem=s_carry.at[0],
            recv_sem=s_carry.at[1],
            device_id=at(1, e, h),
            device_id_type=MESH,
        )

    def row_copy(i):
        return pltpu.make_async_remote_copy(
            src_ref=row_send,
            dst_ref=row_recv.at[h],
            send_sem=s_row_send.at[i],
            recv_sem=s_row_recv.at[h],
            device_id=at(1, e, (h + i) % 2),
            device_id_type=MESH,
        )

    def stat_copy(t):
        return pltpu.make_async_remote_copy(
            src_ref=stat_send.at[t],
            dst_ref=stat_recv.at[t],
            send_sem=s_stat_send.at[t],
            recv_sem=s_stat_recv.at[t],
            device_id=at(s, e, 1 - h),
            device_id_type=MESH,
        )

    load_held.wait()
    pl.semaphore_wait(barrier, 17)
    greet(1, s_here.at[0])
    take_input(held, 0)
    ids_0.start()

    @pl.when(s == 0)
    def _():
        ids_1.start()
        ids_2.start()
        ids_3.start()
        load_fresh.wait()
        take_input(fresh, 1)

    @pl.when(s == 1)
    def _():
        load_fresh.wait()

    load_keys.wait()
    pl.semaphore_wait(s_here.at[0], 3)
    greet(2, s_here.at[1])

    def send_dispatch(t):
        @pl.loop(1, 2 * EXP)
        def _(m):
            e2, h2 = ahead(m)
            j = m // 2
            pltpu.make_async_remote_copy(
                src_ref=send_d.at[t, pl.ds(pl.multiple_of(e2 * MSG, MSG), MSG)],
                dst_ref=recv_d.at[t, j // 4, h, pl.ds(pl.multiple_of((j % 4) * MSG, MSG), MSG)],
                send_sem=s_d_send.at[t, m],
                recv_sem=s_d_recv.at[t, j // 4],
                device_id=at(s, e2, h2),
                device_id_type=MESH,
            ).start()

        pltpu.make_async_copy(
            send_d.at[t, pl.ds(pl.multiple_of(e * MSG, MSG), MSG)],
            recv_d.at[t, 0, h, pl.ds(0, MSG)],
            s_d_recv.at[t, 0],
        ).start()
    def lay_out_weights():
        @pl.loop(0, D // WROWS)
        def _(i):
            load_in(i).wait()
            rows = pl.ds(pl.multiple_of(i * WROWS, WROWS), WROWS)
            w_in[rows, :] = w_part[i % 2].reshape(WROWS, 2 * HID)

            @pl.when(i + 2 < D // WROWS)
            def _():
                load_in(i + 2).start()

        load_out.wait()

    def attention_stage(t):
        @pl.when((t == 1) & (s == 1))
        def _():
            carry_copy().wait_recv()
            for i in range(2):
                pltpu.make_async_remote_copy(
                    src_ref=row_send,
                    dst_ref=row_recv.at[i],
                    send_sem=s_row_send.at[i],
                    recv_sem=s_row_recv.at[i],
                    device_id=at(1, e, h),
                    device_id_type=MESH,
                ).wait_recv()
            total = row_recv[0] + row_recv[1]
            norm(1, lax.rsqrt(jnp.sum(total, axis=1, keepdims=True) * (1.0 / D) + EPS), NCH)
            ids_2.wait_recv()

        chosen = routes[t]
        label = lax.broadcasted_iota(jnp.int32, (EXP, TOK), 0)
        first = (label == chosen[0:1]).astype(F32)
        second = (label == chosen[1:2]).astype(F32)
        ranking = jnp.dot((first + second).astype(BF), before[...], preferred_element_type=F32)
        place_0 = jnp.sum((ranking + label.astype(F32) * CAP) * first, axis=0, keepdims=True)
        place_1 = jnp.sum((ranking + label.astype(F32) * CAP) * second, axis=0, keepdims=True)

        @pl.loop(0, ROWS // TOK)
        def _(r):
            rows = pl.ds(pl.multiple_of(r * TOK, TOK), TOK)
            keys = key_col[rows, :]
            for c in range(NCH):
                hit = (keys == place_0 + 1024.0 * c) | (keys == place_1 + 1024.0 * c)
                pick[rows, c * TOK : (c + 1) * TOK] = hit.astype(F32).astype(BF)

        @pl.when(t == 0)
        def _():
            ids_0.wait_recv()

        @pl.when(t == 1)
        def _():
            ids_1.wait_recv()

        row_ids = jnp.broadcast_to(ids_own[t, 0:1, :].astype(F32), (TOK, TOK))
        prior_ids = jnp.broadcast_to(ids_pri[t, 0:1, :].astype(F32), (TOK, TOK))
        col_ids = jnp.transpose(row_ids)
        causal = lax.broadcasted_iota(jnp.int32, (TOK, TOK), 1) <= lax.broadcasted_iota(
            jnp.int32, (TOK, TOK), 0
        )
        own_mask = jnp.where((col_ids == row_ids) & causal, 0.0, -1e30)
        pri_mask = jnp.where((col_ids == prior_ids) & (e > 0), 0.0, -1e30)
        sums[...] = jnp.zeros((TOK, TOK), F32)

        @pl.loop(0, NCH)
        def _(quad):
            prior_copy(t, quad, 0).wait_recv()

            rows = pl.ds(pl.multiple_of(quad * TOK, TOK), TOK)
            for i in range(4):
                c = quad * 4 + i
                own = normed[t, :, head_cols(c)]
                pri = prior[t, :, head_cols(c)]
                q_gain = query_gain[:, own_cols(c)].astype(F32)
                k_gain = key_gain[:, own_cols(c)].astype(F32)
                queries = (own.astype(F32) * q_gain).astype(BF)
                own_keys = (own.astype(F32) * k_gain).astype(BF)
                pri_keys = (pri.astype(F32) * k_gain).astype(BF)
                dims = (((1,), (1,)), ((), ()))
                own_s = lax.dot_general(queries, own_keys, dims, preferred_element_type=F32)
                pri_s = lax.dot_general(queries, pri_keys, dims, preferred_element_type=F32)
                own_s = own_s * TOK**-0.5 + own_mask
                pri_s = pri_s * TOK**-0.5 + pri_mask
                top = jnp.max(jnp.maximum(own_s, pri_s), axis=1, keepdims=True)
                own_p = jnp.exp(own_s - top)
                pri_p = jnp.exp(pri_s - top)
                total = jnp.sum(own_p + pri_p, axis=1, keepdims=True)
                share = 1.0 / total
                mixed = jnp.dot((own_p * share).astype(BF), own, preferred_element_type=F32)
                mixed += jnp.dot((pri_p * share).astype(BF), pri, preferred_element_type=F32)
                summed = cur[t, :, head_cols(c)].astype(F32) + mixed.astype(BF).astype(F32)
                res[t, :, head_cols(c)] = summed
                sums[...] += summed * summed
                f_gain = ffn_gain[:, own_cols(c)].astype(F32)
                moe[rows, i * TOK : (i + 1) * TOK] = (summed * f_gain).astype(BF)

        stat_send[t, 0:TOK, :] = sums[...]
        part = jnp.zeros((EXP, TOK), F32)
        for c in range(NCH):
            part += lax.dot_general(
                router[:, pl.ds(pl.multiple_of(start_col + c * CH, CH), CH)],
                moe[c * TOK : (c + 1) * TOK, :],
                (((1,), (1,)), ((), ())),
                preferred_element_type=F32,
            )
        stat_send[t, TOK:, :] = part
        stat_copy(t).start()
        stat_copy(t).wait_recv()
        sums[...] = stat_send[t, 0:TOK, :] + stat_recv[t, 0:TOK, :]
        logits = stat_send[t, TOK:, :] + stat_recv[t, TOK:, :]
        scale = lax.rsqrt(jnp.sum(sums[...], axis=1, keepdims=True) * (1.0 / D) + EPS)

        @pl.loop(0, NCH)
        def _(quad):
            rows = pl.ds(pl.multiple_of(quad * TOK, TOK), TOK)
            for i in range(4):
                c = quad * 4 + i
                f_gain = ffn_gain[:, own_cols(c)].astype(F32)
                moe[rows, i * TOK : (i + 1) * TOK] = (
                    res[t, :, head_cols(c)] * scale * f_gain
                ).astype(BF)

        @pl.loop(0, EXP // 4)
        def _(g):
            rows = pl.ds(pl.multiple_of(g * QUAD, QUAD), QUAD)
            send_d[t, rows, :] = jnp.dot(
                pick[rows, :], moe[...], preferred_element_type=F32
            ).astype(BF)

        @pl.when(t == 0)
        def _():
            pl.semaphore_wait(s_here.at[1], 3)

        @pl.when((s == 1) & (t == 0))
        def _():
            lay_out_weights()

        @pl.when((s == 1) | (t == 0))
        def _():
            send_dispatch(t)

        @pl.when((s == 0) & (t == 0))
        def _():
            lay_out_weights()

        @pl.when((s == 1) & (t == 1))
        def _():
            send_all_results(0)

        scale_row = jnp.transpose(jnp.broadcast_to(scale, (TOK, TOK)))
        logits = logits * scale_row[0:EXP, :]
        logit_0 = jnp.sum(logits * first, axis=0, keepdims=True)
        logit_1 = jnp.sum(logits * second, axis=0, keepdims=True)
        top = jnp.maximum(logit_0, logit_1)
        raised_0, raised_1 = jnp.exp(logit_0 - top), jnp.exp(logit_1 - top)

        def column(row):
            return jnp.transpose(jnp.broadcast_to(row, (TOK, TOK)))

        columns[t, 0] = column(raised_0 / (raised_0 + raised_1))
        columns[t, 1] = column(raised_1 / (raised_0 + raised_1))
        columns[t, 2] = column(place_0)
        columns[t, 3] = column(place_1)

    def expert_stage(t):
        @pl.loop(0, 2)
        def _(block):
            @pl.loop(0, 4)
            def _(i):
                g = block * 4 + i
                pltpu.make_async_copy(
                    recv_d.at[t, g], recv_d.at[t, g], s_d_recv.at[t, g]
                ).wait()
                for p in range(2):
                    sorted_rows = jnp.dot(
                        sort[...], recv_d[t, g, p], preferred_element_type=F32
                    ).astype(BF)
                    for c in range(NCH):
                        rows_in[
                            pl.ds(pl.multiple_of(i * 48, 48), 48),
                            p * HALF + c * CH : p * HALF + (c + 1) * CH,
                        ] = sorted_rows[c * 48 : (c + 1) * 48]

            @pl.loop(0, HID // 256)
            def _(n):
                gate = jnp.dot(
                    rows_in[...],
                    w_in[:, pl.ds(pl.multiple_of(n * 256, 256), 256)],
                    preferred_element_type=F32,
                )
                up = jnp.dot(
                    rows_in[...],
                    w_in[:, pl.ds(pl.multiple_of(HID + n * 256, 256), 256)],
                    preferred_element_type=F32,
                )
                inner[:, pl.ds(pl.multiple_of(n * 256, 256), 256)] = (
                    gate / (1.0 + jnp.exp(-gate)) * up
                ).astype(BF)

            @pl.loop(0, 2)
            def _(p):
                for c in range(NCH):
                    col = pl.multiple_of(p * HALF + c * CH, CH)
                    staged[c] = jnp.dot(
                        inner[...], w_out[:, pl.ds(col, CH)], preferred_element_type=F32
                    ).astype(BF)

                @pl.loop(0, 4)
                def _(i):
                    g = block * 4 + i
                    rows = pl.ds(pl.multiple_of(i * 48, 48), 48)
                    stack = staged[:, rows, :].reshape(QUAD, CH)
                    packed = jnp.dot(unsort[...], stack, preferred_element_type=F32)
                    send_c[t, p, pl.ds(pl.multiple_of(g * QUAD, QUAD), QUAD), :] = packed.astype(BF)

                    @pl.when((s == 0) | (t == 1))
                    def _():
                        send_results(t, p, g)

        @pl.when((s == 0) & (t == 0))
        def _():
            send_dispatch(1)

    def send_all_results(t):
        @pl.loop(0, 2)
        def _(p):
            @pl.loop(0, EXP // 4)
            def _(g):
                send_results(t, p, g)

    def send_results(t, p, g):
        @pl.loop(0, 4)
        def _(i):
            j = g * 4 + i
            remote = (j > 0) | (p != h)
            src = send_c.at[t, p, pl.ds(pl.multiple_of(j * MSG, MSG), MSG)]
            dst = recv_c.at[t, h, pl.ds(pl.multiple_of(e * MSG, MSG), MSG)]

            @pl.when(remote)
            def _():
                m = jnp.where(j > 0, j * 2 + p, 1)
                pltpu.make_async_remote_copy(
                    src_ref=src,
                    dst_ref=dst,
                    send_sem=s_c_send.at[t, m],
                    recv_sem=s_c_recv.at[t],
                    device_id=at(s, behind(j), p),
                    device_id_type=MESH,
                ).start()

            @pl.when(jnp.logical_not(remote))
            def _():
                pltpu.make_async_copy(src, dst, s_c_recv.at[t]).start()

    def combine_stage(t):
        @pl.loop(0, ROWS // TOK)
        def _(r):
            cols = pl.ds(pl.multiple_of(r * TOK, TOK), TOK)
            keys = key_row[0:1, cols]
            for c in range(NCH):
                value = jnp.where(keys == columns[t, 2] + 1024.0 * c, columns[t, 0], 0.0)
                value += jnp.where(keys == columns[t, 3] + 1024.0 * c, columns[t, 1], 0.0)
                comb[c, :, cols] = value.astype(BF)

        pltpu.make_async_copy(recv_c.at[t], recv_c.at[t], s_c_recv.at[t]).wait()
        total = jnp.zeros((TOK, TOK), F32)
        for c in range(NCH):
            combined = jnp.dot(comb[c], recv_c[t, 0], preferred_element_type=F32)
            combined += jnp.dot(comb[c], recv_c[t, 1], preferred_element_type=F32)
            final = (res[t, :, c * CH : (c + 1) * CH] + combined).astype(BF)
            out_half[t, :, c * CH : (c + 1) * CH] = final
            for i in range(CH // TOK):
                wide = final[:, i * TOK : (i + 1) * TOK].astype(F32)
                total = total + wide * wide

            @pl.when(t == 1)
            def _():
                far_out(1, c).start()

        @pl.when((t == 0) & (s == 0))
        def _():
            carry_copy().start()
            row_send[...] = total
            for i in range(2):
                row_copy(i).start()

        @pl.when(t == 0)
        def _():
            for c in range(NCH):
                far_out(0, c).start()

        near_out(t).start()

    def near_out(t):
        return pltpu.make_async_copy(
            out_half.at[t], out_hbm.at[t, :, pl.ds(start_col, HALF)], s_out.at[t]
        )

    def far_out(t, c):
        return pltpu.make_async_remote_copy(
            src_ref=out_half.at[t, :, pl.ds(c * CH, CH)],
            dst_ref=out_hbm.at[t, :, pl.ds(pl.multiple_of(start_col + c * CH, CH), CH)],
            send_sem=s_out_send.at[t, c],
            recv_sem=s_out_recv.at[t, c],
            device_id=at(s, e, 1 - h),
            device_id_type=MESH,
        )

    @pl.loop(0, 6)
    def _(step):
        @pl.when((step == 0) | (step == 1 + s))
        def _():
            attention_stage((step + 1) // 2)

        @pl.when((step == 2 - s) | (step == 4 - s))
        def _():
            expert_stage(step // 3)

        @pl.when((step == 3 + s) | (step == 5))
        def _():
            combine_stage(step // 5)

    @pl.loop(0, 2)
    def _(t):
        near_out(t).wait()
        for c in range(NCH):
            far_out(t, c).wait()
        for piece in range(NCH):
            prior_copy(t, piece, 0).wait_send()
        stat_copy(t).wait_send()

    @pl.loop(1, 2 * EXP)
    def _(m):
        for t in range(2):
            pltpu.make_async_remote_copy(
                src_ref=send_c.at[0, 0, pl.ds(0, MSG)],
                dst_ref=recv_c.at[0, 0, pl.ds(0, MSG)],
                send_sem=s_c_send.at[t, m],
                recv_sem=s_c_recv.at[0],
                device_id=at(s, nxt, h),
                device_id_type=MESH,
            ).wait_send()
            pltpu.make_async_remote_copy(
                src_ref=send_d.at[0, pl.ds(0, MSG)],
                dst_ref=recv_d.at[0, 0, 0, pl.ds(0, MSG)],
                send_sem=s_d_send.at[t, m],
                recv_sem=s_d_recv.at[0, 0],
                device_id=at(s, nxt, h),
                device_id_type=MESH,
            ).wait_send()

    ids_0.wait_send()

    @pl.when(s == 0)
    def _():
        ids_1.wait_send()
        ids_2.wait_send()
        ids_3.wait_send()
        carry_copy().wait_send()
        for i in range(2):
            row_copy(i).wait_send()


def body(
    hidden_held,
    fresh_rows,
    doc_held,
    doc_fresh,
    routes,
    attn_gain,
    query_gain,
    key_gain,
    ffn_gain,
    router,
    weight_in,
    weight_out,
):
    key_col, key_row, sort, unsort, before = _constants()
    vmem = pl.BlockSpec(memory_space=pltpu.VMEM)
    hbm = pl.BlockSpec(memory_space=pl.ANY)
    dma = pltpu.SemaphoreType.DMA
    out = pl.pallas_call(
        _kernel,
        out_shape=jax.ShapeDtypeStruct((2, TOK, D), BF),
        in_specs=[hbm] * 2 + [vmem] * 8 + [hbm] * 3 + [vmem] * 4,
        out_specs=hbm,
        scratch_shapes=[
            pltpu.VMEM((TOK, D), BF),
            pltpu.VMEM((TOK, D), BF),
            pltpu.VMEM((ROWS, TOK), F32),
            pltpu.VMEM((2, WROWS, 2, HID), BF),
            pltpu.VMEM((D, 2 * HID), BF),
            pltpu.VMEM((HID, D), BF),
            pltpu.VMEM((2, EXP // 4, 2, QUAD, CH), BF),
            pltpu.VMEM((2, 2, ROWS, CH), BF),
            pltpu.VMEM((2, ROWS, CH), BF),
            pltpu.VMEM((2, 2, ROWS, CH), BF),
            pltpu.VMEM((SLOTS // 2, D), BF),
            pltpu.VMEM((SLOTS // 2, HID), BF),
            pltpu.VMEM((NCH, SLOTS // 2, CH), BF),
            pltpu.VMEM((ROWS, NCH * TOK), BF),
            pltpu.VMEM((NCH, TOK, ROWS), BF),
            pltpu.VMEM((2, TOK, HALF), BF),
            pltpu.VMEM((2, TOK, HALF), BF),
            pltpu.VMEM((2, TOK, HALF // 2), BF),
            pltpu.VMEM((2, TOK, HALF), BF),
            pltpu.VMEM((2, TOK, HALF), F32),
            pltpu.VMEM((NCH * TOK, CH), BF),
            pltpu.VMEM((2, TOK, HALF), BF),
            pltpu.VMEM((TOK, TOK), F32),
            pltpu.VMEM((2, TOK + EXP, TOK), F32),
            pltpu.VMEM((2, TOK + EXP, TOK), F32),
            pltpu.VMEM((TOK, TOK), F32),
            pltpu.VMEM((2, TOK, TOK), F32),
            pltpu.VMEM((2, 4, TOK, TOK), F32),
            pltpu.VMEM((2, 8, TOK), jnp.int32),
            pltpu.VMEM((2, 8, TOK), jnp.int32),
            dma((3,)),
            dma((3,)),
            dma((4,)),
            dma((3,)),
            dma((2, NCH)),
            dma((2, NCH)),
            dma((2,)),
            dma((2,)),
            dma((2,)),
            dma((2,)),
            dma((2,)),
            dma((2, 2 * EXP)),
            dma((2, EXP // 4)),
            dma((2, 2 * EXP)),
            dma((2,)),
            dma((2,)),
            dma((2, NCH)),
            dma((2, NCH)),
            pltpu.SemaphoreType.REGULAR((2,)),
        ],
        compiler_params=pltpu.CompilerParams(
            collective_id=0, has_side_effects=True, vmem_limit_bytes=62 << 20
        ),
        cost_estimate=pl.CostEstimate(
            flops=25_000_000_000, bytes_accessed=25_000_000, transcendentals=5_000_000
        ),
    )(
        hidden_held[0],
        fresh_rows[0],
        doc_held,
        doc_fresh,
        jnp.swapaxes(routes[:, 0], 1, 2),
        attn_gain,
        query_gain,
        key_gain,
        ffn_gain,
        router[0].T,
        weight_in[0, 0],
        weight_out[0, 0],
        jnp.asarray(key_col),
        jnp.asarray(key_row),
        jnp.asarray(sort, BF),
        jnp.asarray(unsort, BF),
        jnp.asarray(before, BF),
    )
    return out[:, None]


def solution(mesh):
    in_specs = (
        P("section", "expert", None),
        P(None, "expert", None),
        P("section", "expert"),
        P(None, "expert"),
        P(None, "section", "expert", None),
        P("section", None),
        P("section", None),
        P("section", None),
        P("section", None),
        P("section", None, None),
        P("section", "expert", None, None, "dp"),
        P("section", "expert", "dp", None),
    )
    out_specs = P(None, "section", "expert", None)
    return jax.shard_map(body, mesh=mesh, in_specs=in_specs, out_specs=out_specs, check_vma=False)
```

```python
import jax
import jax.numpy as jnp
import numpy as np
from jax import lax
from jax.experimental import pallas as pl
from jax.experimental.pallas import tpu as pltpu
from jax.sharding import PartitionSpec as P

MESH = pl.DeviceIdType.MESH
BF = jnp.bfloat16
F32 = jnp.float32
TOK = 128
D = 4096
HALF = 2048
CH = 512
NCH = HALF // CH
EXP = 32
CAP = 12
MSG = CAP * NCH
ROWS = EXP * MSG
QUAD = 4 * MSG
SLOTS = EXP * CAP
HID = 768
WROWS = 256
EPS = 1e-06


def _constants():
    row = np.arange(ROWS)
    chunk = (row % MSG) // CAP
    key = (row // MSG) * CAP + row % CAP + 1024 * chunk
    key_col = np.broadcast_to(key[:, None], (ROWS, TOK)).astype(np.float32)
    key_row = np.broadcast_to(key[None, :], (8, ROWS)).astype(np.float32)
    sort = np.zeros((QUAD, QUAD), np.float32)
    for j in range(4):
        for c in range(NCH):
            for slot in range(CAP):
                sort[c * 48 + j * CAP + slot, j * MSG + c * CAP + slot] = 1.0
    before = np.triu(np.ones((TOK, TOK), np.float32), 1)
    return key_col, key_row, sort, sort.T.copy(), before


def _kernel(
    held_hbm,
    fresh_hbm,
    ids_held,
    ids_fresh,
    routes,
    attn_gain,
    query_gain,
    key_gain,
    ffn_gain,
    router,
    w_in_hbm,
    w_out_hbm,
    key_col_hbm,
    key_row,
    sort,
    unsort,
    before,
    out_hbm,
    held,
    fresh,
    key_col,
    w_part,
    w_in,
    w_out,
    recv_d,
    recv_c,
    send_d,
    send_c,
    rows_in,
    inner,
    staged,
    pick,
    comb,
    cur,
    normed,
    far,
    prior,
    res,
    moe,
    out_half,
    sums,
    stat_send,
    stat_recv,
    row_send,
    row_recv,
    columns,
    ids_own,
    ids_pri,
    s_w,
    s_in,
    s_ids_send,
    s_ids_recv,
    s_prior_send,
    s_prior_recv,
    s_stat_send,
    s_stat_recv,
    s_carry,
    s_row_send,
    s_row_recv,
    s_d_send,
    s_d_recv,
    s_c_send,
    s_c_recv,
    s_out,
    s_out_send,
    s_out_recv,
    s_here,
):
    s = lax.axis_index("section")
    e = lax.axis_index("expert")
    h = lax.axis_index("dp")
    z, y, xl = e // 8, (e // 2) % 4, e % 2
    x = h * 2 + xl
    start_col = pl.multiple_of(h * HALF, HALF)

    def at(section, expert, dp):
        return {"section": section, "expert": expert, "dp": dp}

    def offset(j):
        k = (13 * j) % 32
        return k % 2, (k // 2) % 4, k // 8

    def ahead(m):
        dx, dy, dz = offset(m // 2)
        x2 = (x + dx + 2 * (m % 2)) % 4
        return ((z + dz) % 4) * 8 + ((y + dy) % 4) * 2 + x2 % 2, x2 // 2

    def behind(j):
        dx, dy, dz = offset(j)
        return ((z + 4 - dz) % 4) * 8 + ((y + 4 - dy) % 4) * 2 + (xl + dx) % 2

    nxt, prv = (e + 1) % EXP, (e + EXP - 1) % EXP

    load_held = pltpu.make_async_copy(held_hbm, held, s_in.at[0])
    load_fresh = pltpu.make_async_copy(fresh_hbm, fresh, s_in.at[1])
    load_keys = pltpu.make_async_copy(key_col_hbm, key_col, s_in.at[2])
    load_held.start()
    barrier = pltpu.get_barrier_semaphore()

    def along(axis, i):
        if axis == 0:
            x2 = (x + i) % 4
            return at(s, e - xl + x2 % 2, x2 // 2)
        if axis == 1:
            return at(s, z * 8 + ((y + i) % 4) * 2 + xl, h)
        return at(s, ((z + i) % 4) * 8 + y * 2 + xl, h)

    def greet(axis, sem):
        for i in range(1, 4):
            pl.semaphore_signal(sem, inc=1, device_id=along(axis, i), device_id_type=MESH)

    for e2 in (nxt, prv):
        for h2 in (h, 1 - h):
            pl.semaphore_signal(barrier, inc=1, device_id=at(s, e2, h2), device_id_type=MESH)
    for e2, h2 in ((e, h), (e, 1 - h), (nxt, h), (prv, h)):
        pl.semaphore_signal(barrier, inc=1, device_id=at(1 - s, e2, h2), device_id_type=MESH)
    for axis in range(3):
        greet(axis, barrier)

    load_keys.start()
    load_fresh.start()
    load_out = pltpu.make_async_copy(w_out_hbm, w_out, s_w.at[2])
    load_out.start()

    def load_in(i):
        return pltpu.make_async_copy(
            w_in_hbm.at[pl.ds(i * WROWS, WROWS)], w_part.at[i % 2], s_w.at[i % 2]
        )

    load_in(0).start()
    load_in(1).start()

    ids_own[0] = jnp.broadcast_to(ids_held[...], (8, TOK))

    @pl.when(s == 0)
    def _():
        ids_own[1] = jnp.broadcast_to(ids_fresh[...], (8, TOK))

    def send_ids(src, dst, i, j, device):
        return pltpu.make_async_remote_copy(
            src_ref=src,
            dst_ref=dst,
            send_sem=s_ids_send.at[i],
            recv_sem=s_ids_recv.at[j],
            device_id=device,
            device_id_type=MESH,
        )

    ids_0 = send_ids(ids_own.at[0], ids_pri.at[0], 0, 0, at(s, nxt, h))
    ids_1 = send_ids(ids_own.at[1], ids_pri.at[1], 1, 1, at(0, nxt, h))
    ids_2 = send_ids(ids_own.at[0], ids_own.at[1], 2, 2, at(1, e, h))
    ids_3 = send_ids(ids_own.at[0], ids_pri.at[1], 3, 1, at(1, nxt, h))
    def head_cols(c):
        return pl.ds(pl.multiple_of(c * TOK, TOK), TOK)

    def own_cols(c):
        return pl.ds(pl.multiple_of(start_col + c * TOK, TOK), TOK)

    def take_input(ref, t):
        def add(i, total):
            for j in range(8):
                wide = ref[:, head_cols(i * 8 + j)].astype(F32)
                total = total + wide * wide
            return total

        total = lax.fori_loop(0, D // TOK // 8, add, jnp.zeros((TOK, TOK), F32))
        scale = lax.rsqrt(jnp.sum(total, axis=1, keepdims=True) * (1.0 / D) + EPS)
        cur[t] = ref[:, pl.ds(start_col, HALF)]
        far_col = pl.multiple_of((1 - h) * HALF + HALF // 2, HALF // 2)

        norm(t, scale, 2)
        for piece in range(2):
            for j in range(4):
                c = piece * 4 + j
                cols = pl.ds(pl.multiple_of(far_col + c * TOK, TOK), TOK)
                wide = ref[:, cols].astype(F32)
                gain = attn_gain[:, cols].astype(F32)
                far[t, :, head_cols(c)] = (wide * scale * gain).astype(BF)
            prior_copy(t, 2 + piece, 1).start()

    def norm(t, scale, sent):
        for piece in range(NCH):
            for i in range(4):
                c = piece * 4 + i
                wide = cur[t, :, head_cols(c)].astype(F32)
                gain = attn_gain[:, own_cols(c)].astype(F32)
                normed[t, :, head_cols(c)] = (wide * scale * gain).astype(BF)
            if piece < sent:
                prior_copy(t, piece, 0).start()

    def prior_copy(t, piece, across):
        cols = pl.ds(piece * CH, CH)
        return pltpu.make_async_remote_copy(
            src_ref=far.at[t, :, pl.ds(piece * CH - HALF // 2, CH)]
            if across
            else normed.at[t, :, cols],
            dst_ref=prior.at[t, :, cols],
            send_sem=s_prior_send.at[t, piece],
            recv_sem=s_prior_recv.at[t, piece],
            device_id=at(s, nxt, 1 - h if across else h),
            device_id_type=MESH,
        )

    def carry_copy():
        return pltpu.make_async_remote_copy(
            src_ref=out_half.at[0],
            dst_ref=cur.at[1],
            send_sem=s_carry.at[0],
            recv_sem=s_carry.at[1],
            device_id=at(1, e, h),
            device_id_type=MESH,
        )

    def row_copy(i):
        return pltpu.make_async_remote_copy(
            src_ref=row_send,
            dst_ref=row_recv.at[h],
            send_sem=s_row_send.at[i],
            recv_sem=s_row_recv.at[h],
            device_id=at(1, e, (h + i) % 2),
            device_id_type=MESH,
        )

    def stat_copy(t):
        return pltpu.make_async_remote_copy(
            src_ref=stat_send.at[t],
            dst_ref=stat_recv.at[t],
            send_sem=s_stat_send.at[t],
            recv_sem=s_stat_recv.at[t],
            device_id=at(s, e, 1 - h),
            device_id_type=MESH,
        )

    def lay_out_weights():
        @pl.loop(0, D // WROWS)
        def _(i):
            load_in(i).wait()
            rows = pl.ds(pl.multiple_of(i * WROWS, WROWS), WROWS)
            w_in[rows, :] = w_part[i % 2].reshape(WROWS, 2 * HID)

            @pl.when(i + 2 < D // WROWS)
            def _():
                load_in(i + 2).start()

        load_out.wait()

    load_held.wait()
    pl.semaphore_wait(barrier, 17)
    greet(1, s_here.at[0])

    @pl.when(s == 1)
    def _():
        lay_out_weights()

    take_input(held, 0)
    ids_0.start()

    @pl.when(s == 0)
    def _():
        ids_1.start()
        ids_2.start()
        ids_3.start()
        load_fresh.wait()
        take_input(fresh, 1)

    @pl.when(s == 1)
    def _():
        load_fresh.wait()

    load_keys.wait()
    pl.semaphore_wait(s_here.at[0], 3)
    greet(2, s_here.at[1])

    def send_dispatch(t):
        @pl.loop(1, 2 * EXP)
        def _(m):
            e2, h2 = ahead(m)
            j = m // 2
            pltpu.make_async_remote_copy(
                src_ref=send_d.at[t, pl.ds(pl.multiple_of(e2 * MSG, MSG), MSG)],
                dst_ref=recv_d.at[t, j // 4, h, pl.ds(pl.multiple_of((j % 4) * MSG, MSG), MSG)],
                send_sem=s_d_send.at[t, m],
                recv_sem=s_d_recv.at[t, j // 4],
                device_id=at(s, e2, h2),
                device_id_type=MESH,
            ).start()

        pltpu.make_async_copy(
            send_d.at[t, pl.ds(pl.multiple_of(e * MSG, MSG), MSG)],
            recv_d.at[t, 0, h, pl.ds(0, MSG)],
            s_d_recv.at[t, 0],
        ).start()
    def attention_stage(t):
        @pl.when((t == 1) & (s == 1))
        def _():
            carry_copy().wait_recv()
            for i in range(2):
                pltpu.make_async_remote_copy(
                    src_ref=row_send,
                    dst_ref=row_recv.at[i],
                    send_sem=s_row_send.at[i],
                    recv_sem=s_row_recv.at[i],
                    device_id=at(1, e, h),
                    device_id_type=MESH,
                ).wait_recv()
            total = row_recv[0] + row_recv[1]
            norm(1, lax.rsqrt(jnp.sum(total, axis=1, keepdims=True) * (1.0 / D) + EPS), NCH)
            ids_2.wait_recv()

        chosen = routes[t]
        label = lax.broadcasted_iota(jnp.int32, (EXP, TOK), 0)
        first = (label == chosen[0:1]).astype(F32)
        second = (label == chosen[1:2]).astype(F32)
        ranking = jnp.dot((first + second).astype(BF), before[...], preferred_element_type=F32)
        place_0 = jnp.sum((ranking + label.astype(F32) * CAP) * first, axis=0, keepdims=True)
        place_1 = jnp.sum((ranking + label.astype(F32) * CAP) * second, axis=0, keepdims=True)

        @pl.loop(0, ROWS // TOK)
        def _(r):
            rows = pl.ds(pl.multiple_of(r * TOK, TOK), TOK)
            keys = key_col[rows, :]
            for c in range(NCH):
                hit = (keys == place_0 + 1024.0 * c) | (keys == place_1 + 1024.0 * c)
                pick[rows, c * TOK : (c + 1) * TOK] = hit.astype(F32).astype(BF)

        @pl.when(t == 0)
        def _():
            ids_0.wait_recv()

        @pl.when(t == 1)
        def _():
            ids_1.wait_recv()

        row_ids = jnp.broadcast_to(ids_own[t, 0:1, :].astype(F32), (TOK, TOK))
        prior_ids = jnp.broadcast_to(ids_pri[t, 0:1, :].astype(F32), (TOK, TOK))
        col_ids = jnp.transpose(row_ids)
        causal = lax.broadcasted_iota(jnp.int32, (TOK, TOK), 1) <= lax.broadcasted_iota(
            jnp.int32, (TOK, TOK), 0
        )
        own_mask = jnp.where((col_ids == row_ids) & causal, 0.0, -1e30)
        pri_mask = jnp.where((col_ids == prior_ids) & (e > 0), 0.0, -1e30)
        sums[...] = jnp.zeros((TOK, TOK), F32)

        @pl.loop(0, NCH)
        def _(quad):
            prior_copy(t, quad, 0).wait_recv()

            rows = pl.ds(pl.multiple_of(quad * TOK, TOK), TOK)
            for i in range(4):
                c = quad * 4 + i
                own = normed[t, :, head_cols(c)]
                pri = prior[t, :, head_cols(c)]
                q_gain = query_gain[:, own_cols(c)].astype(F32)
                k_gain = key_gain[:, own_cols(c)].astype(F32)
                queries = (own.astype(F32) * q_gain).astype(BF)
                own_keys = (own.astype(F32) * k_gain).astype(BF)
                pri_keys = (pri.astype(F32) * k_gain).astype(BF)
                dims = (((1,), (1,)), ((), ()))
                own_s = lax.dot_general(queries, own_keys, dims, preferred_element_type=F32)
                pri_s = lax.dot_general(queries, pri_keys, dims, preferred_element_type=F32)
                own_s = own_s * TOK**-0.5 + own_mask
                pri_s = pri_s * TOK**-0.5 + pri_mask
                top = jnp.max(jnp.maximum(own_s, pri_s), axis=1, keepdims=True)
                own_p = jnp.exp(own_s - top)
                pri_p = jnp.exp(pri_s - top)
                total = jnp.sum(own_p + pri_p, axis=1, keepdims=True)
                share = 1.0 / total
                mixed = jnp.dot((own_p * share).astype(BF), own, preferred_element_type=F32)
                mixed += jnp.dot((pri_p * share).astype(BF), pri, preferred_element_type=F32)
                summed = cur[t, :, head_cols(c)].astype(F32) + mixed.astype(BF).astype(F32)
                res[t, :, head_cols(c)] = summed
                sums[...] += summed * summed
                f_gain = ffn_gain[:, own_cols(c)].astype(F32)
                moe[rows, i * TOK : (i + 1) * TOK] = (summed * f_gain).astype(BF)

        stat_send[t, 0:TOK, :] = sums[...]
        part = jnp.zeros((EXP, TOK), F32)
        for c in range(NCH):
            part += lax.dot_general(
                router[:, pl.ds(pl.multiple_of(start_col + c * CH, CH), CH)],
                moe[c * TOK : (c + 1) * TOK, :],
                (((1,), (1,)), ((), ())),
                preferred_element_type=F32,
            )
        stat_send[t, TOK:, :] = part
        stat_copy(t).start()
        stat_copy(t).wait_recv()
        sums[...] = stat_send[t, 0:TOK, :] + stat_recv[t, 0:TOK, :]
        logits = stat_send[t, TOK:, :] + stat_recv[t, TOK:, :]
        scale = lax.rsqrt(jnp.sum(sums[...], axis=1, keepdims=True) * (1.0 / D) + EPS)

        @pl.loop(0, NCH)
        def _(quad):
            rows = pl.ds(pl.multiple_of(quad * TOK, TOK), TOK)
            for i in range(4):
                c = quad * 4 + i
                f_gain = ffn_gain[:, own_cols(c)].astype(F32)
                moe[rows, i * TOK : (i + 1) * TOK] = (
                    res[t, :, head_cols(c)] * scale * f_gain
                ).astype(BF)

        @pl.loop(0, EXP // 4)
        def _(g):
            rows = pl.ds(pl.multiple_of(g * QUAD, QUAD), QUAD)
            send_d[t, rows, :] = jnp.dot(
                pick[rows, :], moe[...], preferred_element_type=F32
            ).astype(BF)

        @pl.when(t == 0)
        def _():
            pl.semaphore_wait(s_here.at[1], 3)

        @pl.when((s == 1) | (t == 0))
        def _():
            send_dispatch(t)

        @pl.when((s == 0) & (t == 0))
        def _():
            lay_out_weights()

        scale_row = jnp.transpose(jnp.broadcast_to(scale, (TOK, TOK)))
        logits = logits * scale_row[0:EXP, :]
        logit_0 = jnp.sum(logits * first, axis=0, keepdims=True)
        logit_1 = jnp.sum(logits * second, axis=0, keepdims=True)
        top = jnp.maximum(logit_0, logit_1)
        raised_0, raised_1 = jnp.exp(logit_0 - top), jnp.exp(logit_1 - top)

        def column(row):
            return jnp.transpose(jnp.broadcast_to(row, (TOK, TOK)))

        columns[t, 0] = column(raised_0 / (raised_0 + raised_1))
        columns[t, 1] = column(raised_1 / (raised_0 + raised_1))
        columns[t, 2] = column(place_0)
        columns[t, 3] = column(place_1)

    def expert_stage(t):
        @pl.loop(0, 2)
        def _(block):
            @pl.loop(0, 4)
            def _(i):
                g = block * 4 + i
                pltpu.make_async_copy(
                    recv_d.at[t, g], recv_d.at[t, g], s_d_recv.at[t, g]
                ).wait()
                for p in range(2):
                    sorted_rows = jnp.dot(
                        sort[...], recv_d[t, g, p], preferred_element_type=F32
                    ).astype(BF)
                    for c in range(NCH):
                        rows_in[
                            pl.ds(pl.multiple_of(i * 48, 48), 48),
                            p * HALF + c * CH : p * HALF + (c + 1) * CH,
                        ] = sorted_rows[c * 48 : (c + 1) * 48]

            @pl.when((s == 1) & (t == 1) & (block == 0))
            def _():
                send_all_results(0)

            @pl.loop(0, HID // 256)
            def _(n):
                gate = jnp.dot(
                    rows_in[...],
                    w_in[:, pl.ds(pl.multiple_of(n * 256, 256), 256)],
                    preferred_element_type=F32,
                )
                up = jnp.dot(
                    rows_in[...],
                    w_in[:, pl.ds(pl.multiple_of(HID + n * 256, 256), 256)],
                    preferred_element_type=F32,
                )
                inner[:, pl.ds(pl.multiple_of(n * 256, 256), 256)] = (
                    gate / (1.0 + jnp.exp(-gate)) * up
                ).astype(BF)

            @pl.loop(0, 2)
            def _(p):
                for c in range(NCH):
                    col = pl.multiple_of(p * HALF + c * CH, CH)
                    staged[c] = jnp.dot(
                        inner[...], w_out[:, pl.ds(col, CH)], preferred_element_type=F32
                    ).astype(BF)

                @pl.loop(0, 4)
                def _(i):
                    g = block * 4 + i
                    rows = pl.ds(pl.multiple_of(i * 48, 48), 48)
                    stack = staged[:, rows, :].reshape(QUAD, CH)
                    packed = jnp.dot(unsort[...], stack, preferred_element_type=F32)
                    send_c[t, p, pl.ds(pl.multiple_of(g * QUAD, QUAD), QUAD), :] = packed.astype(BF)

                    @pl.when((s == 0) | (t == 1))
                    def _():
                        send_results(t, p, g)

        @pl.when((s == 0) & (t == 0))
        def _():
            send_dispatch(1)

        @pl.when((s == 0) & (t == 1))
        def _():
            for c in range(NCH):
                far_out(0, c).start()

    def send_all_results(t):
        @pl.loop(0, 2)
        def _(p):
            @pl.loop(0, EXP // 4)
            def _(g):
                send_results(t, p, g)

    def send_results(t, p, g):
        @pl.loop(0, 4)
        def _(i):
            j = g * 4 + i
            remote = (j > 0) | (p != h)
            src = send_c.at[t, p, pl.ds(pl.multiple_of(j * MSG, MSG), MSG)]
            dst = recv_c.at[t, h, pl.ds(pl.multiple_of(e * MSG, MSG), MSG)]

            @pl.when(remote)
            def _():
                m = jnp.where(j > 0, j * 2 + p, 1)
                pltpu.make_async_remote_copy(
                    src_ref=src,
                    dst_ref=dst,
                    send_sem=s_c_send.at[t, m],
                    recv_sem=s_c_recv.at[t],
                    device_id=at(s, behind(j), p),
                    device_id_type=MESH,
                ).start()

            @pl.when(jnp.logical_not(remote))
            def _():
                pltpu.make_async_copy(src, dst, s_c_recv.at[t]).start()

    def combine_stage(t):
        @pl.loop(0, ROWS // TOK)
        def _(r):
            cols = pl.ds(pl.multiple_of(r * TOK, TOK), TOK)
            keys = key_row[0:1, cols]
            for c in range(NCH):
                value = jnp.where(keys == columns[t, 2] + 1024.0 * c, columns[t, 0], 0.0)
                value += jnp.where(keys == columns[t, 3] + 1024.0 * c, columns[t, 1], 0.0)
                comb[c, :, cols] = value.astype(BF)

        pltpu.make_async_copy(recv_c.at[t], recv_c.at[t], s_c_recv.at[t]).wait()
        total = jnp.zeros((TOK, TOK), F32)
        for c in range(NCH):
            combined = jnp.dot(comb[c], recv_c[t, 0], preferred_element_type=F32)
            combined += jnp.dot(comb[c], recv_c[t, 1], preferred_element_type=F32)
            final = (res[t, :, c * CH : (c + 1) * CH] + combined).astype(BF)
            out_half[t, :, c * CH : (c + 1) * CH] = final
            for i in range(CH // TOK):
                wide = final[:, i * TOK : (i + 1) * TOK].astype(F32)
                total = total + wide * wide

            @pl.when(t == 1)
            def _():
                far_out(1, c).start()

        @pl.when((t == 0) & (s == 0))
        def _():
            carry_copy().start()
            row_send[...] = total
            for i in range(2):
                row_copy(i).start()

        @pl.when((t == 0) & (s == 1))
        def _():
            for c in range(NCH):
                far_out(0, c).start()

        near_out(t).start()

    def near_out(t):
        return pltpu.make_async_copy(
            out_half.at[t], out_hbm.at[t, :, pl.ds(start_col, HALF)], s_out.at[t]
        )

    def far_out(t, c):
        return pltpu.make_async_remote_copy(
            src_ref=out_half.at[t, :, pl.ds(c * CH, CH)],
            dst_ref=out_hbm.at[t, :, pl.ds(pl.multiple_of(start_col + c * CH, CH), CH)],
            send_sem=s_out_send.at[t, c],
            recv_sem=s_out_recv.at[t, c],
            device_id=at(s, e, 1 - h),
            device_id_type=MESH,
        )

    @pl.loop(0, 6)
    def _(step):
        @pl.when((step == 0) | (step == 1 + s))
        def _():
            attention_stage((step + 1) // 2)

        @pl.when((step == 2 - s) | (step == 4 - s))
        def _():
            expert_stage(step // 3)

        @pl.when((step == 3 + s) | (step == 5))
        def _():
            combine_stage(step // 5)

    @pl.loop(0, 2)
    def _(t):
        near_out(t).wait()
        for c in range(NCH):
            far_out(t, c).wait()
        for piece in range(NCH):
            prior_copy(t, piece, 0).wait_send()
        stat_copy(t).wait_send()

    @pl.loop(1, 2 * EXP)
    def _(m):
        for t in range(2):
            pltpu.make_async_remote_copy(
                src_ref=send_c.at[0, 0, pl.ds(0, MSG)],
                dst_ref=recv_c.at[0, 0, pl.ds(0, MSG)],
                send_sem=s_c_send.at[t, m],
                recv_sem=s_c_recv.at[0],
                device_id=at(s, nxt, h),
                device_id_type=MESH,
            ).wait_send()
            pltpu.make_async_remote_copy(
                src_ref=send_d.at[0, pl.ds(0, MSG)],
                dst_ref=recv_d.at[0, 0, 0, pl.ds(0, MSG)],
                send_sem=s_d_send.at[t, m],
                recv_sem=s_d_recv.at[0, 0],
                device_id=at(s, nxt, h),
                device_id_type=MESH,
            ).wait_send()

    ids_0.wait_send()

    @pl.when(s == 0)
    def _():
        ids_1.wait_send()
        ids_2.wait_send()
        ids_3.wait_send()
        carry_copy().wait_send()
        for i in range(2):
            row_copy(i).wait_send()


def body(
    hidden_held,
    fresh_rows,
    doc_held,
    doc_fresh,
    routes,
    attn_gain,
    query_gain,
    key_gain,
    ffn_gain,
    router,
    weight_in,
    weight_out,
):
    key_col, key_row, sort, unsort, before = _constants()
    vmem = pl.BlockSpec(memory_space=pltpu.VMEM)
    hbm = pl.BlockSpec(memory_space=pl.ANY)
    dma = pltpu.SemaphoreType.DMA
    out = pl.pallas_call(
        _kernel,
        out_shape=jax.ShapeDtypeStruct((2, TOK, D), BF),
        in_specs=[hbm] * 2 + [vmem] * 8 + [hbm] * 3 + [vmem] * 4,
        out_specs=hbm,
        scratch_shapes=[
            pltpu.VMEM((TOK, D), BF),
            pltpu.VMEM((TOK, D), BF),
            pltpu.VMEM((ROWS, TOK), F32),
            pltpu.VMEM((2, WROWS, 2, HID), BF),
            pltpu.VMEM((D, 2 * HID), BF),
            pltpu.VMEM((HID, D), BF),
            pltpu.VMEM((2, EXP // 4, 2, QUAD, CH), BF),
            pltpu.VMEM((2, 2, ROWS, CH), BF),
            pltpu.VMEM((2, ROWS, CH), BF),
            pltpu.VMEM((2, 2, ROWS, CH), BF),
            pltpu.VMEM((SLOTS // 2, D), BF),
            pltpu.VMEM((SLOTS // 2, HID), BF),
            pltpu.VMEM((NCH, SLOTS // 2, CH), BF),
            pltpu.VMEM((ROWS, NCH * TOK), BF),
            pltpu.VMEM((NCH, TOK, ROWS), BF),
            pltpu.VMEM((2, TOK, HALF), BF),
            pltpu.VMEM((2, TOK, HALF), BF),
            pltpu.VMEM((2, TOK, HALF // 2), BF),
            pltpu.VMEM((2, TOK, HALF), BF),
            pltpu.VMEM((2, TOK, HALF), F32),
            pltpu.VMEM((NCH * TOK, CH), BF),
            pltpu.VMEM((2, TOK, HALF), BF),
            pltpu.VMEM((TOK, TOK), F32),
            pltpu.VMEM((2, TOK + EXP, TOK), F32),
            pltpu.VMEM((2, TOK + EXP, TOK), F32),
            pltpu.VMEM((TOK, TOK), F32),
            pltpu.VMEM((2, TOK, TOK), F32),
            pltpu.VMEM((2, 4, TOK, TOK), F32),
            pltpu.VMEM((2, 8, TOK), jnp.int32),
            pltpu.VMEM((2, 8, TOK), jnp.int32),
            dma((3,)),
            dma((3,)),
            dma((4,)),
            dma((3,)),
            dma((2, NCH)),
            dma((2, NCH)),
            dma((2,)),
            dma((2,)),
            dma((2,)),
            dma((2,)),
            dma((2,)),
            dma((2, 2 * EXP)),
            dma((2, EXP // 4)),
            dma((2, 2 * EXP)),
            dma((2,)),
            dma((2,)),
            dma((2, NCH)),
            dma((2, NCH)),
            pltpu.SemaphoreType.REGULAR((2,)),
        ],
        compiler_params=pltpu.CompilerParams(
            collective_id=0, has_side_effects=True, vmem_limit_bytes=62 << 20
        ),
        cost_estimate=pl.CostEstimate(
            flops=25_000_000_000, bytes_accessed=25_000_000, transcendentals=5_000_000
        ),
    )(
        hidden_held[0],
        fresh_rows[0],
        doc_held,
        doc_fresh,
        jnp.swapaxes(routes[:, 0], 1, 2),
        attn_gain,
        query_gain,
        key_gain,
        ffn_gain,
        router[0].T,
        weight_in[0, 0],
        weight_out[0, 0],
        jnp.asarray(key_col),
        jnp.asarray(key_row),
        jnp.asarray(sort, BF),
        jnp.asarray(unsort, BF),
        jnp.asarray(before, BF),
    )
    return out[:, None]


def solution(mesh):
    in_specs = (
        P("section", "expert", None),
        P(None, "expert", None),
        P("section", "expert"),
        P(None, "expert"),
        P(None, "section", "expert", None),
        P("section", None),
        P("section", None),
        P("section", None),
        P("section", None),
        P("section", None, None),
        P("section", "expert", None, None, "dp"),
        P("section", "expert", "dp", None),
    )
    out_specs = P(None, "section", "expert", None)
    return jax.shard_map(body, mesh=mesh, in_specs=in_specs, out_specs=out_specs, check_vma=False)
```
